128 devices in a mesh: ctx: 32 (over z_lo, x, y), head: 4 (over z_hi, core).
Axes of the slice: x: 4, y: 4, z: 4 (z_hi: 2, z_lo: 2; z = z_hi * 2 + z_lo), core: 2. Of those that a mesh axis runs over, the one named last changes fastest.
Arguments:
- queries: bfloat16 [4096, 12288], P('ctx', 'head'), may hold values from -230 to 230
- latents: bfloat16 [576, 4096], P(None, 'ctx'), may hold values from -6 to 6
- w_key: bfloat16 [64, 128, 512], P('head'), may hold values from -0.5 to 0.5
- w_value: bfloat16 [64, 512, 128], P('head'), may hold values from -0.25 to 0.25
- w_out: bfloat16 [8192, 3584], P('head'), may hold values from -0.0625 to 0.0625
- block_order: int32 [32], replicated, may hold values from 0 to 31, each once
Outputs:
- attended: bfloat16 [3584, 4096], P('head', 'ctx')
The draws below stay inside these ranges and needn't reach their ends.
All inputs are finite; a program needn't handle non-finite values.
Results may differ from the reference program's by a relative error of at most 0.017.
Values may be sent and summed in bfloat16 or wider, within the bound.
A program may use at most 192 MiB of HBM per device.

```python
import math
import jax
import jax.numpy as jnp
from jax import lax

H = 64
NOPE = 128
R = 64
C = 512
V = 128
D = 3584
TOK_DEV = 128
TOKENS = 4096
N_CTX = 32


def shared_keys(key):
    return jnp.clip(jax.random.normal(key, (C + R, TOKENS), jnp.float32), -4.5, 4.5)


def draw_latents(key, part):
    base = shared_keys(key)
    return base.astype(jnp.bfloat16)


def draw_queries(key, part):
    key = jax.random.fold_in(key, 9)
    values = jnp.clip(jax.random.normal(key, (TOKENS, H, NOPE + R), jnp.float32), -4.5, 4.5)
    return values.reshape(TOKENS, H * (NOPE + R)).astype(jnp.bfloat16)


def block_scale(key, extent, split, smallest, largest):
    loudness, own = 1.0, jax.random.fold_in(key, 6)
    for axis_at, shards_of in split:
        draws = jnp.exp(jax.random.uniform(jax.random.fold_in(own, axis_at), (shards_of,), jnp.float32, smallest / len(split), largest / len(split)))
        loudness = loudness * jnp.repeat(draws, extent[axis_at] // shards_of).reshape([-1 if axis == axis_at else 1 for axis in range(len(extent))])
    return loudness


def gaussian(own_key, dims, spread, bound, cuts=(), kind=jnp.bfloat16):
    values = jax.random.normal(own_key, dims, jnp.float32) * spread
    if len(cuts) > 0:
        values = block_scale(own_key, dims, cuts, -0.22, 0.18) * values
    return jnp.clip(values, min=-bound, max=bound).astype(kind)


def setup_inputs(seed: int = 0) -> dict:
    key_list = jax.random.split(jax.random.key(seed), 7)
    queries = draw_queries(jax.random.fold_in(key_list[6], 71), 0)
    latents = draw_latents(jax.random.fold_in(key_list[6], 71), 0)
    w_key = gaussian(key_list[2], (H, NOPE, C), NOPE ** -0.5, 0.5, ((0, 4),))
    w_value = gaussian(key_list[3], (H, C, V), C ** -0.5, 0.25, ((0, 4),))
    w_out = gaussian(key_list[4], (H * V, D), (H * V) ** -0.5, 0.0625, ((0, 4),))
    block_order = jax.random.permutation(key_list[5], N_CTX).astype(jnp.int32)
    return dict(queries=queries, latents=latents, w_key=w_key, w_value=w_value, w_out=w_out, block_order=block_order)


NEG = -1e+30

def reference(queries, latents, w_key, w_value, w_out, block_order):
    rows = jnp.arange(TOKENS, dtype=jnp.int32)
    positions = (block_order[rows // TOK_DEV] * TOK_DEV + rows % TOK_DEV).astype(jnp.int32)
    order = jnp.argsort(positions).astype(jnp.int32)
    sorted_q = jnp.take(queries, order, axis=0)
    sorted_kv = jnp.take(latents, order, axis=1)
    scale = 1.0 / math.sqrt(NOPE + R)
    width = min(512, TOKENS)
    outputs = []
    for first in range(0, TOKENS, width):
        end = first + width
        block_q = jnp.transpose(sorted_q[first:end].reshape(width, H, NOPE + R), (1, 0, 2))
        keys = sorted_kv[:, :end]
        query_pos = first + jnp.arange(width, dtype=jnp.int32)
        key_pos = jnp.arange(end, dtype=jnp.int32)
        visible = key_pos[None, :] <= query_pos[:, None]

        def one_head(items):
            query_head, key_proj, value_proj = items
            absorbed = jnp.dot(query_head[:, :NOPE], key_proj, preferred_element_type=jnp.float32).astype(jnp.bfloat16)
            query_cat = jnp.concatenate([absorbed, query_head[:, NOPE:]], axis=1)
            score = jnp.dot(query_cat, keys, preferred_element_type=jnp.float32) * scale
            score = jnp.where(visible, score, NEG)
            top = lax.optimization_barrier(jnp.max(score, axis=1, keepdims=True))
            expo = jnp.where(visible, jnp.exp(score - top), 0.0)
            total = lax.optimization_barrier(jnp.sum(expo, axis=1, keepdims=True))
            summed = lax.dot_general(expo.astype(jnp.bfloat16), keys[:C], (((1,), (1,)), ((), ())), preferred_element_type=jnp.float32)
            mixed = (summed / total).astype(jnp.bfloat16)
            return jnp.dot(mixed, value_proj, preferred_element_type=jnp.float32).astype(jnp.bfloat16)
        heads_done = lax.map(one_head, (block_q, w_key, w_value))
        joined = jnp.transpose(heads_done, (1, 0, 2)).reshape(width, H * V)
        outputs.append(jnp.dot(joined, w_out, preferred_element_type=jnp.float32))
    result = jnp.concatenate(outputs, axis=0)
    return jnp.take(result, positions, axis=0).T.astype(jnp.bfloat16)
```

```python
import functools
import math

import jax
import jax.numpy as jnp
from jax import lax
from jax.experimental import pallas as pl
from jax.experimental.pallas import tpu as pltpu
from jax.sharding import PartitionSpec as P

NOPE = 128
R = 64
C = 512
V = 128
HEADS = 16
SPAN = 128
ROWS = HEADS * SPAN
BLOCKS = 32
KDIM = 640
TILE = 256
OWN_D = 896
NEG = -1e30
EXP_SCALE = math.log2(math.e) / math.sqrt(NOPE + R)
MESH = pl.DeviceIdType.MESH
F32 = jnp.float32
BF16 = jnp.bfloat16

CHUNKS = (
    ((0, 0),),
    ((1, 0), (3, 0), (0, 1), (0, 3)),
    ((2, 0), (1, 1), (1, 3), (3, 1)),
    ((3, 3), (2, 1), (2, 3), (0, 2)),
    ((1, 2), (2, 2), (3, 2)),
)


def slot_table():
    mine, other, bounds, at = {}, {}, [], 0
    for group in CHUNKS:
        first = at
        for table in (mine, other):
            for offset in group:
                table[offset] = at
                at += 1
        bounds.append((first, at))
    return mine, other, bounds


MINE, OTHER, BOUNDS = slot_table()
HALF_SEM = BLOCKS
N_RECV = BLOCKS + 1
N_SEND = 40


def kernel(
    q_hbm, lat_hbm, wk_hbm, wv_hbm, wo_hbm, order_ref, out_ref,
    q_ref, wk_ref, wv_ref, wo_ref, qc_ref, k_ref, kt_ref, mask_ref,
    m_ref, l_ref, acc_ref, s_ref, p_ref, a_ref, ho_ref,
    send_a, recv_a, send_b, recv_b, send_c, recv_c,
    load_sem, send_sem, recv_sem, rs_send, rs_recv,
):
    ci, hi = lax.axis_index("ctx"), lax.axis_index("head")
    z_lo, x, y = lax.div(ci, 16), lax.rem(lax.div(ci, 4), 4), lax.rem(ci, 4)
    z_hi, core = lax.div(hi, 2), lax.rem(hi, 2)
    sibling = (ci, z_hi * 2 + 1 - core)
    partner = (ci, (1 - z_hi) * 2 + core)
    z_near = ((1 - z_lo) * 16 + x * 4 + y, ((1 - core) * (1 - z_hi) + core * z_hi) * 2 + core)

    def place(along_core, z_low, du, dv):
        nx = lax.rem(x + (1 - along_core) * du + along_core * dv, 4)
        ny = lax.rem(y + (1 - along_core) * dv + along_core * du, 4)
        return z_low * 16 + nx * 4 + ny

    def at(du, dv):
        return (place(core, z_lo, du, dv), hi)

    around = [at(1, 0), at(3, 0), at(0, 1), at(0, 3)]

    def cols(slot):
        return pl.ds(slot * SPAN, SPAN) if isinstance(slot, int) else pl.ds(pl.multiple_of(slot * SPAN, SPAN), SPAN)

    def slab(slot, first=0, rows=C + R):
        return k_ref.at[pl.ds(first, rows), cols(slot)]

    sends = {}

    def send(src, dst, sem, device, rows=C + R):
        number = sends.setdefault(sem, (len(sends), rows))[0]
        pltpu.make_async_remote_copy(
            src_ref=src, dst_ref=dst, send_sem=send_sem.at[number], recv_sem=recv_sem.at[sem],
            device_id=device, device_id_type=MESH,
        ).start()

    def arrived(slot):
        pltpu.make_async_copy(slab(slot), slab(slot), recv_sem.at[slot]).wait()

    def arrived_half(first, sem):
        pltpu.make_async_copy(slab(0, first, 288), slab(0, first, 288), recv_sem.at[sem]).wait()

    def relay(offset):
        send(slab(MINE[offset]), slab(OTHER[offset]), OTHER[offset], sibling)

    def onward(src, dst, du, dv):
        send(slab(MINE[src]), slab(MINE[dst]), MINE[dst], at(du, dv))

    loads = [
        pltpu.make_async_copy(q_hbm, q_ref, load_sem.at[0]),
        pltpu.make_async_copy(wk_hbm, wk_ref, load_sem.at[1]),
        pltpu.make_async_copy(wv_hbm, wv_ref, load_sem.at[2]),
        pltpu.make_async_copy(wo_hbm, wo_ref, load_sem.at[3]),
    ]
    own_slot = core
    own_copy = pltpu.make_async_copy(lat_hbm, slab(own_slot), recv_sem.at[own_slot])
    own_copy.start()
    loads[0].start()
    loads[1].start()

    barrier = pltpu.get_barrier_semaphore()
    greeted = around + [sibling, partner, z_near]
    for device in greeted:
        pl.semaphore_signal(barrier, inc=1, device_id=device, device_id_type=MESH)
    pl.semaphore_wait(barrier, len(greeted))

    z_slot = 1 - core
    pltpu.make_async_remote_copy(
        src_ref=lat_hbm, dst_ref=slab(z_slot), send_sem=rs_send.at[3], recv_sem=recv_sem.at[z_slot],
        device_id=z_near, device_id_type=MESH,
    ).start()
    loads[2].start()
    loads[3].start()

    here = order_ref[ci]
    first_row = lax.broadcasted_iota(jnp.int32, (KDIM - C - R, SPAN), 0) == 0
    for group in CHUNKS:
        for table, along, z_low in (
            (MINE, core, (1 - core) * z_lo + core * (1 - z_lo)),
            (OTHER, 1 - core, core * z_lo + (1 - core) * (1 - z_lo)),
        ):
            for offset in group:
                block = order_ref[place(along, z_low, *offset)]
                bias = jnp.where(block <= here, 0.0, NEG)
                k_ref[C + R:, cols(table[offset])] = jnp.where(first_row, bias, 0.0).astype(BF16)
    token = lax.rem(lax.broadcasted_iota(jnp.int32, (TILE, 2 * SPAN), 0), SPAN)
    key = lax.broadcasted_iota(jnp.int32, (TILE, 2 * SPAN), 1)
    hidden = (lax.div(key, SPAN) == core) & (lax.rem(key, SPAN) > token)
    mask_ref[...] = jnp.where(hidden, NEG, 0.0)

    def spread():
        arrived(0)
        send(slab(0), slab(MINE[(3, 0)]), MINE[(3, 0)], around[0])
        send(slab(0), slab(MINE[(1, 0)]), MINE[(1, 0)], around[1])
        send(slab(0), slab(MINE[(0, 3)]), MINE[(0, 3)], around[2])
        send(slab(0), slab(MINE[(0, 1)]), MINE[(0, 1)], around[3])

    loads[0].wait()
    loads[1].wait()
    lane = lax.broadcasted_iota(jnp.int32, (SPAN, R), 1)
    one = jnp.where(lane == 0, 1.0, 0.0).astype(BF16)
    for h in range(HEADS):
        base = h * (NOPE + R)
        rows = slice(h * SPAN, (h + 1) * SPAN)
        qc_ref[rows, :C] = jnp.dot(
            q_ref[:, base:base + NOPE], wk_ref[h], preferred_element_type=F32
        ).astype(BF16)
        qc_ref[rows, C:] = jnp.concatenate([q_ref[:, base + NOPE:base + NOPE + R], one], axis=1)
    spread()
    arrived(1)

    tiles = ROWS // TILE

    def chunk(index, events):
        first, last = BOUNDS[index]
        width = (last - first) * SPAN
        keys = slice(first * SPAN, last * SPAN)
        begin = index == 0

        def rows_of(t):
            return pl.ds(t * TILE, TILE) if isinstance(t, int) else pl.ds(pl.multiple_of(t * TILE, TILE), TILE)

        def scores(t, b):
            s = jnp.dot(qc_ref[rows_of(t), :], k_ref[:, keys], preferred_element_type=F32)
            if begin:
                s = s + mask_ref[...]
            s_ref[b, :, :width] = s

        def soft(t, b):
            r = rows_of(t)
            s = s_ref[b, :, :width]
            top = jnp.max(s, axis=1, keepdims=True) * EXP_SCALE
            if begin:
                m_new = jnp.broadcast_to(top, (TILE, 128))
            else:
                m_old = m_ref[r, :]
                m_new = jnp.maximum(m_old, top)
                alpha = jnp.exp2(m_old - m_new)
                a_ref[b] = alpha
            wide = jnp.concatenate([m_new] * (width // 128), axis=1)
            e = jnp.exp2(s * EXP_SCALE - wide)
            part = e[:, :128]
            for i in range(1, width // 128):
                part = part + e[:, i * 128:(i + 1) * 128]
            l_ref[r, :] = part if begin else l_ref[r, :] * alpha + part
            m_ref[r, :] = m_new
            p_ref[b, :, :width] = e.astype(BF16)

        def values(t, b):
            r = rows_of(t)
            add = jnp.dot(p_ref[b, :, :width], kt_ref[:width, :], preferred_element_type=F32)
            if begin:
                acc_ref[r, :] = add
            else:
                acc_ref[r, :] = acc_ref[r, :] * jnp.concatenate([a_ref[b]] * 4, axis=1) + add

        kt_ref[:width, :] = k_ref[:C, keys].T
        scores(0, 0)
        scores(1, 1)
        soft(0, 0)

        def body(u, carry):
            for step, event in events.items():
                pl.when(u == step)(event)
            t = 2 * u + 2
            scores(t, 0)
            soft(t - 1, 1)
            values(t - 2, 0)
            scores(t + 1, 1)
            soft(t, 0)
            values(t - 1, 1)
            return carry

        lax.fori_loop(0, (tiles - 2) // 2, body, 0)
        soft(tiles - 1, 1)
        values(tiles - 2, 0)
        values(tiles - 1, 1)

    def others(index):
        for offset in CHUNKS[index]:
            arrived(OTHER[offset])

    chunk(0, {})

    arrived(MINE[(1, 0)])
    relay((1, 0))
    arrived(MINE[(3, 0)])
    relay((3, 0))
    send(slab(MINE[(3, 0)], 0, 288), slab(MINE[(2, 0)], 0, 288), MINE[(2, 0)], around[0], 288)
    send(slab(MINE[(1, 0)], 288, 288), slab(MINE[(2, 0)], 288, 288), HALF_SEM, around[1], 288)
    for du in (1, 3):
        onward((du, 0), (du, 3), 0, 1)
        onward((du, 0), (du, 1), 0, 3)
    arrived(MINE[(0, 1)])
    relay((0, 1))
    arrived(MINE[(0, 3)])
    relay((0, 3))
    onward((0, 3), (0, 2), 0, 1)
    others(1)

    def line_end():
        arrived_half(0, MINE[(2, 0)])
        arrived_half(288, HALF_SEM)
        relay((2, 0))
        onward((2, 0), (2, 3), 0, 1)
        onward((2, 0), (2, 1), 0, 3)

    def second():
        for offset in ((1, 1), (1, 3), (3, 1)):
            arrived(MINE[offset])
            relay(offset)
        onward((1, 3), (1, 2), 0, 1)
        onward((3, 1), (3, 2), 0, 3)

    def third():
        for offset in ((3, 3), (2, 1), (2, 3), (0, 2)):
            arrived(MINE[offset])
            relay(offset)
        onward((2, 1), (2, 2), 0, 3)

    def fourth():
        for offset in CHUNKS[4]:
            arrived(MINE[offset])
            relay(offset)

    chunk(1, {0: line_end, 2: second})
    others(2)
    chunk(2, {2: third})
    others(3)
    chunk(3, {1: fourth})
    others(4)
    chunk(4, {})

    loads[2].wait()
    for h in range(HEADS):
        rows = slice(h * SPAN, (h + 1) * SPAN)
        total = jnp.sum(l_ref[rows, :], axis=1, keepdims=True)
        mixed = (acc_ref[rows, :] / total).astype(BF16)
        ho_ref[:, h * V:(h + 1) * V] = jnp.dot(mixed, wv_ref[h], preferred_element_type=F32).astype(BF16)
    loads[3].wait()

    def project(zh, c):
        at_col = pl.multiple_of((zh * 2 + c) * OWN_D, 128)
        return jnp.dot(ho_ref[...], wo_ref[:, pl.ds(at_col, OWN_D)], preferred_element_type=F32)

    def rs(src, dst, n, device):
        copy = pltpu.make_async_remote_copy(
            src_ref=src, dst_ref=dst, send_sem=rs_send.at[n], recv_sem=rs_recv.at[n],
            device_id=device, device_id_type=MESH,
        )
        copy.start()
        return copy

    send_a[...] = project(1 - z_hi, 1 - core).astype(BF16)
    copy_a = rs(send_a, recv_a, 0, sibling)
    s_ref[0, :SPAN, :OWN_D] = project(1 - z_hi, core)
    copy_a.wait()
    send_b[...] = (s_ref[0, :SPAN, :OWN_D] + recv_a[...].astype(F32)).astype(BF16)
    copy_b = rs(send_b, recv_b, 1, partner)
    send_c[...] = project(z_hi, 1 - core).astype(BF16)
    copy_c = rs(send_c, recv_c, 2, sibling)
    s_ref[1, :SPAN, :OWN_D] = project(z_hi, core)
    copy_c.wait()
    s_ref[1, :SPAN, :OWN_D] = s_ref[1, :SPAN, :OWN_D] + recv_c[...].astype(F32)
    pltpu.make_async_copy(lat_hbm, lat_hbm, rs_send.at[3]).wait()
    for number, rows in sends.values():
        pltpu.make_async_copy(slab(0, 0, rows), slab(0, 0, rows), send_sem.at[number]).wait()
    copy_b.wait()
    out_ref[...] = (s_ref[1, :SPAN, :OWN_D] + recv_b[...].astype(F32)).T.astype(BF16)


def shards(queries, latents, w_key, w_value, w_out, block_order):
    any_spec = pl.BlockSpec(memory_space=pl.ANY)
    flops = 2 * ROWS * BLOCKS * SPAN * (KDIM + C)
    return pl.pallas_call(
        kernel,
        out_shape=jax.ShapeDtypeStruct((OWN_D, SPAN), BF16),
        in_specs=[any_spec] * 5 + [pl.BlockSpec(memory_space=pltpu.SMEM)],
        out_specs=pl.BlockSpec(memory_space=pltpu.VMEM),
        scratch_shapes=[
            pltpu.VMEM((SPAN, HEADS * (NOPE + R)), BF16),
            pltpu.VMEM((HEADS, NOPE, C), BF16),
            pltpu.VMEM((HEADS, C, V), BF16),
            pltpu.VMEM((HEADS * V, 4 * OWN_D), BF16),
            pltpu.VMEM((ROWS, KDIM), BF16),
            pltpu.VMEM((KDIM, BLOCKS * SPAN), BF16),
            pltpu.VMEM((1024, C), BF16),
            pltpu.VMEM((TILE, 2 * SPAN), F32),
            pltpu.VMEM((ROWS, 128), F32),
            pltpu.VMEM((ROWS, 128), F32),
            pltpu.VMEM((ROWS, C), F32),
            pltpu.VMEM((2, TILE, 1024), F32),
            pltpu.VMEM((2, TILE, 1024), BF16),
            pltpu.VMEM((2, TILE, 128), F32),
            pltpu.VMEM((SPAN, HEADS * V), BF16),
        ] + [pltpu.VMEM((SPAN, OWN_D), BF16)] * 6 + [
            pltpu.SemaphoreType.DMA((4,)),
            pltpu.SemaphoreType.DMA((N_SEND,)),
            pltpu.SemaphoreType.DMA((N_RECV,)),
            pltpu.SemaphoreType.DMA((4,)),
            pltpu.SemaphoreType.DMA((3,)),
        ],
        compiler_params=pltpu.CompilerParams(
            collective_id=0, has_side_effects=True, vmem_limit_bytes=58 * 2**20
        ),
        cost_estimate=pl.CostEstimate(flops=flops, bytes_accessed=20 * 2**20, transcendentals=ROWS * BLOCKS * SPAN),
        name="latent_attention",
    )(queries, latents, w_key, w_value, w_out, block_order)


def solution(mesh):
    return jax.shard_map(
        shards,
        mesh=mesh,
        in_specs=(
            P("ctx", "head"),
            P(None, "ctx"),
            P("head", None, None),
            P("head", None, None),
            P("head", None),
            P(),
        ),
        out_specs=P("head", "ctx"),
        check_vma=False,
    )
```

```python
import functools
import math

import jax
import jax.numpy as jnp
from jax import lax
from jax.experimental import pallas as pl
from jax.experimental.pallas import tpu as pltpu
from jax.sharding import PartitionSpec as P

NOPE = 128
R = 64
C = 512
V = 128
HEADS = 16
SPAN = 128
ROWS = HEADS * SPAN
BLOCKS = 32
KDIM = 640
TILE = 512
OWN_D = 896
NEG = -1e30
EXP_SCALE = math.log2(math.e) / math.sqrt(NOPE + R)
MESH = pl.DeviceIdType.MESH
F32 = jnp.float32
BF16 = jnp.bfloat16

FETCHED = ("10", "30", "20", "13", "31", "21", "23")
CHUNKS = (
    ("OWN",),
    ("Z00", "M10", "M30"),
    ("O10", "O30", "M20", "O20"),
    ("M13", "M31", "MZ10", "MZ30"),
    ("O13", "O31", "OZ10", "OZ30", "M21", "M23", "O21", "O23"),
    ("P22", "MZ20", "OZ20", "MZ13", "MZ31", "OZ13", "OZ31", "MZ21"),
    ("MZ23", "OZ21", "OZ23", "Z22"),
)
ORDER = [name for group in CHUNKS for name in group]
SLOT = {name: number for number, name in enumerate(ORDER)}
P22_HALF, Z22_HALF = BLOCKS, BLOCKS + 1
N_RECV = BLOCKS + 2
N_SEND = 48
HALF = (C + R) // 2


def kernel(
    q_hbm, lat_hbm, wk_hbm, wv_hbm, wo_hbm, order_ref, out_ref,
    q_ref, wk_ref, wv_ref, wo_ref, qc_ref, k_ref, kt_ref, mask_ref,
    m_ref, l_ref, acc_ref, s_ref, p_ref, a_ref, ho_ref,
    send_a, recv_a, send_b, recv_b, send_c, recv_c,
    load_sem, send_sem, recv_sem, rs_send, rs_recv,
):
    ci, hi = lax.axis_index("ctx"), lax.axis_index("head")
    z_lo, x, y = lax.div(ci, 16), lax.rem(lax.div(ci, 4), 4), lax.rem(ci, 4)
    z_hi, core = lax.div(hi, 2), lax.rem(hi, 2)
    sibling = (ci, z_hi * 2 + 1 - core)
    partner = (ci, (1 - z_hi) * 2 + core)
    z_near = ((1 - z_lo) * 16 + x * 4 + y, ((1 - core) * (1 - z_hi) + core * z_hi) * 2 + core)

    def place(along_core, z_low, du, dw):
        nx = lax.rem(x + (1 - along_core) * du + along_core * dw, 4)
        ny = lax.rem(y + (1 - along_core) * (4 - dw) + along_core * du, 4)
        return z_low * 16 + nx * 4 + ny

    def at(du, dw):
        return (place(core, z_lo, du, dw), hi)

    def source(name):
        if name == "OWN":
            return ci
        z_low = 1 - z_lo if "Z" in name else z_lo
        along = 1 - core if "O" in name else core
        return place(along, z_low, int(name[-2]), int(name[-1]))

    def cols(slot):
        return pl.ds(slot * SPAN, SPAN)

    def slab(name, first=0, rows=C + R):
        return k_ref.at[pl.ds(first, rows), cols(SLOT[name])]

    half_at = pl.multiple_of(core * HALF, 32)

    def half(name):
        return slab(name, half_at, HALF)

    sends = {}

    def send(src, dst, key, sem, device, rows=C + R):
        number = sends.setdefault(key, (len(sends), rows))[0]
        pltpu.make_async_remote_copy(
            src_ref=src, dst_ref=dst, send_sem=send_sem.at[number], recv_sem=recv_sem.at[sem],
            device_id=device, device_id_type=MESH,
        ).start()

    def arrived(*names):
        for name in names:
            pltpu.make_async_copy(slab(name), slab(name), recv_sem.at[SLOT[name]]).wait()

    def arrived_half(sem):
        pltpu.make_async_copy(half("OWN"), half("OWN"), recv_sem.at[sem]).wait()

    def relay(*names):
        for name in names:
            there = name.replace("M", "O")
            send(slab(name), slab(there), there, SLOT[there], sibling)

    def along_z(*names):
        for name in names:
            there = "MZ" + name[1:]
            send(slab(name), slab(there), there, SLOT[there], z_near)

    def onward(name, there, device):
        send(slab(name), slab(there), there, SLOT[there], device)

    barrier = pltpu.get_barrier_semaphore()
    greeted = [
        at(2, 0), at(0, 2), at(1, 0), at(3, 0), at(0, 1), at(0, 3), z_near, partner, sibling,
    ]
    for device in greeted:
        pl.semaphore_signal(barrier, inc=1, device_id=device, device_id_type=MESH)

    own_copy = pltpu.make_async_copy(lat_hbm, slab("OWN"), load_sem.at[4])
    loads = [
        pltpu.make_async_copy(q_hbm, q_ref, load_sem.at[0]),
        pltpu.make_async_copy(wk_hbm, wk_ref, load_sem.at[1]),
        pltpu.make_async_copy(wv_hbm, wv_ref, load_sem.at[2]),
        pltpu.make_async_copy(wo_hbm, wo_ref, load_sem.at[3]),
    ]
    own_copy.start()
    for load in loads:
        load.start()

    here = order_ref[ci]
    first_row = lax.broadcasted_iota(jnp.int32, (KDIM - C - R, SPAN), 0) == 0
    for name in ORDER:
        bias = jnp.where(order_ref[source(name)] <= here, 0.0, NEG)
        k_ref[C + R:, cols(SLOT[name])] = jnp.where(first_row, bias, 0.0).astype(BF16)
    token = lax.rem(lax.broadcasted_iota(jnp.int32, (TILE, SPAN), 0), SPAN)
    key = lax.broadcasted_iota(jnp.int32, (TILE, SPAN), 1)
    mask_ref[...] = jnp.where(key > token, NEG, 0.0)

    loads[0].wait()
    loads[1].wait()
    lane = lax.broadcasted_iota(jnp.int32, (SPAN, R), 1)
    one = jnp.where(lane == 0, 1.0, 0.0).astype(BF16)
    for h in range(HEADS):
        base = h * (NOPE + R)
        rows = slice(h * SPAN, (h + 1) * SPAN)
        qc_ref[rows, :C] = jnp.dot(
            q_ref[:, base:base + NOPE], wk_ref[h], preferred_element_type=F32
        ).astype(BF16)
        qc_ref[rows, C:] = jnp.concatenate([q_ref[:, base + NOPE:base + NOPE + R], one], axis=1)
    own_copy.wait()

    tiles = ROWS // TILE

    def chunk(index, events=None):
        events = events or {}
        first = SLOT[CHUNKS[index][0]]
        last = first + len(CHUNKS[index])
        width = (last - first) * SPAN
        keys = slice(first * SPAN, last * SPAN)
        begin = index == 0

        def rows_of(t):
            return pl.ds(t * TILE, TILE) if isinstance(t, int) else pl.ds(pl.multiple_of(t * TILE, TILE), TILE)

        def scores(t, b):
            s = jnp.dot(qc_ref[rows_of(t), :], k_ref[:, keys], preferred_element_type=F32)
            if begin:
                s = s + mask_ref[...]
            s_ref[b, :, :width] = s

        def soft(t, b):
            r = rows_of(t)
            s = s_ref[b, :, :width]
            top = jnp.max(s, axis=1, keepdims=True) * EXP_SCALE
            if begin:
                m_new = jnp.broadcast_to(top, (TILE, 128))
            else:
                m_old = m_ref[r, :]
                m_new = jnp.maximum(m_old, top)
                alpha = jnp.exp2(m_old - m_new)
                a_ref[b] = alpha
            wide = jnp.concatenate([m_new] * (width // 128), axis=1)
            e = jnp.exp2(s * EXP_SCALE - wide)
            part = e[:, :128]
            for i in range(1, width // 128):
                part = part + e[:, i * 128:(i + 1) * 128]
            l_ref[r, :] = part if begin else l_ref[r, :] * alpha + part
            m_ref[r, :] = m_new
            p_ref[b, :, :width] = e.astype(BF16)

        def values(t, b):
            r = rows_of(t)
            add = jnp.dot(p_ref[b, :, :width], kt_ref[:width, :], preferred_element_type=F32)
            if begin:
                acc_ref[r, :] = add
            else:
                acc_ref[r, :] = acc_ref[r, :] * jnp.concatenate([a_ref[b]] * 4, axis=1) + add

        kt_ref[:width, :] = k_ref[:C, keys].T
        for step in range(tiles + 2):
            if step in events:
                events[step]()
            if step < tiles:
                scores(step, step % 2)
            if 0 <= step - 1 < tiles:
                soft(step - 1, (step - 1) % 2)
            if 0 <= step - 2 < tiles:
                values(step - 2, step % 2)

    chunk(0)
    pl.semaphore_wait(barrier, len(greeted))
    onward("OWN", "M30", at(1, 0))
    onward("OWN", "M10", at(3, 0))
    onward("OWN", "Z00", z_near)
    onward("OWN", "M20", at(2, 0))

    arrived("M10", "M30")
    relay("M10", "M30")
    onward("M10", "M13", at(0, 1))
    onward("M30", "M31", at(0, 3))
    along_z("M10", "M30")
    arrived("Z00")
    chunk(1)

    arrived("M20")
    relay("M20")
    onward("M20", "M23", at(0, 1))
    onward("M20", "M21", at(0, 3))
    send(half("M20"), half("P22"), "P22", SLOT["P22"], at(0, 2), HALF)
    along_z("M20")
    arrived("O10", "O30", "O20")
    chunk(2)

    arrived("M13", "M31")
    relay("M13", "M31")
    along_z("M13", "M31")
    arrived("MZ10", "MZ30")
    relay("MZ10", "MZ30")

    def third():
        arrived("M21", "M23")
        relay("M21", "M23")
        along_z("M21", "M23")
        arrived_half(SLOT["P22"])
        send(half("P22"), half("P22"), "P22r", P22_HALF, sibling, HALF)
        send(half("P22"), half("Z22"), "Z22", SLOT["Z22"], z_near, HALF)
        arrived("MZ20")
        relay("MZ20")

    chunk(3, {3: third})
    arrived("O13", "O31", "OZ10", "OZ30", "O21", "O23")

    def fourth():
        arrived("MZ13", "MZ31")
        relay("MZ13", "MZ31")

    def fifth():
        arrived("MZ21", "MZ23")
        relay("MZ21", "MZ23")
        arrived_half(SLOT["Z22"])
        send(half("Z22"), half("Z22"), "Z22r", Z22_HALF, sibling, HALF)

    chunk(4, {2: fourth, 4: fifth})
    arrived_half(P22_HALF)
    arrived("OZ20", "OZ13", "OZ31")
    chunk(5)
    arrived_half(Z22_HALF)
    arrived("OZ21", "OZ23")
    chunk(6)

    loads[2].wait()
    for h in range(HEADS):
        rows = slice(h * SPAN, (h + 1) * SPAN)
        total = jnp.sum(l_ref[rows, :], axis=1, keepdims=True)
        mixed = (acc_ref[rows, :] / total).astype(BF16)
        ho_ref[:, h * V:(h + 1) * V] = jnp.dot(mixed, wv_ref[h], preferred_element_type=F32).astype(BF16)
    loads[3].wait()

    pieces = ((0, 512), (512, 384))

    def project(zh, c, piece):
        at_col = pl.multiple_of((zh * 2 + c) * OWN_D + piece[0], 128)
        return jnp.dot(ho_ref[...], wo_ref[:, pl.ds(at_col, piece[1])], preferred_element_type=F32)

    def window(ref, piece):
        return ref.at[:, pl.ds(*piece)]

    def rs(src, dst, n, device):
        copy = pltpu.make_async_remote_copy(
            src_ref=src, dst_ref=dst, send_sem=rs_send.at[n], recv_sem=rs_recv.at[n],
            device_id=device, device_id_type=MESH,
        )
        copy.start()
        return copy

    copies_a, copies_b, copies_c = [], [], []
    for n, piece in enumerate(pieces):
        window(send_a, piece)[...] = project(1 - z_hi, 1 - core, piece).astype(BF16)
        copies_a.append(rs(window(send_a, piece), window(recv_a, piece), n, sibling))
    far = s_ref.at[0, pl.ds(0, SPAN)]
    near = s_ref.at[1, pl.ds(0, SPAN)]
    for piece in pieces:
        window(far, piece)[...] = project(1 - z_hi, core, piece)
    for n, piece in enumerate(pieces):
        window(send_c, piece)[...] = project(z_hi, 1 - core, piece).astype(BF16)
        copies_a[n].wait()
        window(send_b, piece)[...] = (window(far, piece)[...] + window(recv_a, piece)[...].astype(F32)).astype(BF16)
        copies_b.append(rs(window(send_b, piece), window(recv_b, piece), 2 + n, partner))
        copies_c.append(rs(window(send_c, piece), window(recv_c, piece), 4 + n, sibling))
    for piece in pieces:
        window(near, piece)[...] = project(z_hi, core, piece)
    for n, piece in enumerate(pieces):
        copies_c[n].wait()
        window(near, piece)[...] = window(near, piece)[...] + window(recv_c, piece)[...].astype(F32)
    for number, rows in sends.values():
        pltpu.make_async_copy(slab("OWN", 0, rows), slab("OWN", 0, rows), send_sem.at[number]).wait()
    for n, piece in enumerate(pieces):
        copies_b[n].wait()
        out_ref[pl.ds(*piece), :] = (window(near, piece)[...] + window(recv_b, piece)[...].astype(F32)).T.astype(BF16)


def shards(queries, latents, w_key, w_value, w_out, block_order):
    any_spec = pl.BlockSpec(memory_space=pl.ANY)
    flops = 2 * ROWS * BLOCKS * SPAN * (KDIM + C)
    return pl.pallas_call(
        kernel,
        out_shape=jax.ShapeDtypeStruct((OWN_D, SPAN), BF16),
        in_specs=[any_spec] * 5 + [pl.BlockSpec(memory_space=pltpu.SMEM)],
        out_specs=pl.BlockSpec(memory_space=pltpu.VMEM),
        scratch_shapes=[
            pltpu.VMEM((SPAN, HEADS * (NOPE + R)), BF16),
            pltpu.VMEM((HEADS, NOPE, C), BF16),
            pltpu.VMEM((HEADS, C, V), BF16),
            pltpu.VMEM((HEADS * V, 4 * OWN_D), BF16),
            pltpu.VMEM((ROWS, KDIM), BF16),
            pltpu.VMEM((KDIM, BLOCKS * SPAN), BF16),
            pltpu.VMEM((1024, C), BF16),
            pltpu.VMEM((TILE, SPAN), F32),
            pltpu.VMEM((ROWS, 128), F32),
            pltpu.VMEM((ROWS, 128), F32),
            pltpu.VMEM((ROWS, C), F32),
            pltpu.VMEM((2, TILE, 1024), F32),
            pltpu.VMEM((2, TILE, 1024), BF16),
            pltpu.VMEM((2, TILE, 128), F32),
            pltpu.VMEM((SPAN, HEADS * V), BF16),
        ] + [pltpu.VMEM((SPAN, OWN_D), BF16)] * 6 + [
            pltpu.SemaphoreType.DMA((5,)),
            pltpu.SemaphoreType.DMA((N_SEND,)),
            pltpu.SemaphoreType.DMA((N_RECV,)),
            pltpu.SemaphoreType.DMA((6,)),
            pltpu.SemaphoreType.DMA((6,)),
        ],
        compiler_params=pltpu.CompilerParams(
            collective_id=0, has_side_effects=True, vmem_limit_bytes=58 * 2**20
        ),
        cost_estimate=pl.CostEstimate(flops=flops, bytes_accessed=20 * 2**20, transcendentals=ROWS * BLOCKS * SPAN),
        name="latent_attention",
    )(queries, latents, w_key, w_value, w_out, block_order)


def solution(mesh):
    return jax.shard_map(
        shards,
        mesh=mesh,
        in_specs=(
            P("ctx", "head"),
            P(None, "ctx"),
            P("head", None, None),
            P("head", None, None),
            P("head", None),
            P(),
        ),
        out_specs=P("head", "ctx"),
        check_vma=False,
    )
```

```python
import functools
import math

import jax
import jax.numpy as jnp
from jax import lax
from jax.experimental import pallas as pl
from jax.experimental.pallas import tpu as pltpu
from jax.sharding import PartitionSpec as P

NOPE = 128
R = 64
C = 512
V = 128
HEADS = 16
SPAN = 128
ROWS = HEADS * SPAN
BLOCKS = 32
KDIM = 640
TILE = 512
OWN_D = 896
NEG = -1e30
EXP_SCALE = math.log2(math.e) / math.sqrt(NOPE + R)
MESH = pl.DeviceIdType.MESH
F32 = jnp.float32
BF16 = jnp.bfloat16

CHUNKS = (
    ("OWN",),
    ("Z00", "M10", "M30"),
    ("O10", "O30", "M20", "O20"),
    ("M13", "M31", "MZ10", "MZ30"),
    ("O13", "O31", "OZ10", "OZ30", "M21", "M23", "O21", "O23"),
    ("P22", "MZ20", "OZ20", "MZ13", "MZ31", "OZ13", "OZ31", "MZ21"),
    ("MZ23", "OZ21", "OZ23", "Z22"),
)
WIDEST = max(len(group) for group in CHUNKS) * 128
ORDER = [name for group in CHUNKS for name in group]
SLOT = {name: number for number, name in enumerate(ORDER)}
P22_HALF, Z22_HALF = BLOCKS, BLOCKS + 1
N_RECV = BLOCKS + 2
N_SEND = 48
HALF = (C + R) // 2


def kernel(
    q_hbm, lat_hbm, wk_hbm, wv_hbm, wo_hbm, order_ref, out_ref,
    q_ref, wk_ref, wv_ref, wo_ref, qc_ref, k_ref, kt_ref, mask_ref,
    m_ref, l_ref, acc_ref, s_ref, p_ref, a_ref, ho_ref,
    send_a, recv_a, send_b, recv_b, send_c, recv_c,
    load_sem, send_sem, recv_sem, rs_send, rs_recv,
):
    ci, hi = lax.axis_index("ctx"), lax.axis_index("head")
    z_lo, x, y = lax.div(ci, 16), lax.rem(lax.div(ci, 4), 4), lax.rem(ci, 4)
    z_hi, core = lax.div(hi, 2), lax.rem(hi, 2)
    sibling = (ci, z_hi * 2 + 1 - core)
    partner = (ci, (1 - z_hi) * 2 + core)
    z_near = ((1 - z_lo) * 16 + x * 4 + y, ((1 - core) * (1 - z_hi) + core * z_hi) * 2 + core)

    def place(along_core, z_low, du, dw):
        nx = lax.rem(x + (1 - along_core) * du + along_core * dw, 4)
        ny = lax.rem(y + (1 - along_core) * (4 - dw) + along_core * du, 4)
        return z_low * 16 + nx * 4 + ny

    def at(du, dw):
        return (place(core, z_lo, du, dw), hi)

    u_up, u_down, u_far = at(1, 0), at(3, 0), at(2, 0)
    w_up, w_down, w_far = at(0, 1), at(0, 3), at(0, 2)

    def source(name):
        if name == "OWN":
            return ci
        z_low = 1 - z_lo if "Z" in name else z_lo
        along = 1 - core if "O" in name else core
        return place(along, z_low, int(name[-2]), int(name[-1]))

    def cols(slot, count=1):
        return pl.ds(slot * SPAN, count * SPAN)

    def slab(name, first=0, rows=C + R, count=1):
        return k_ref.at[pl.ds(first, rows), cols(SLOT[name], count)]

    half_at = pl.multiple_of(core * HALF, 32)

    def half(name):
        return slab(name, half_at, HALF)

    sends = {}

    def send(src, dst, key, sem, device, rows=C + R, count=1):
        number = sends.setdefault(key, (len(sends), rows, count))[0]
        pltpu.make_async_remote_copy(
            src_ref=src, dst_ref=dst, send_sem=send_sem.at[number], recv_sem=recv_sem.at[sem],
            device_id=device, device_id_type=MESH,
        ).start()

    def arrived(*names):
        for name in names:
            pltpu.make_async_copy(slab(name), slab(name), recv_sem.at[SLOT[name]]).wait()

    def arrived_pair(*names):
        for name in names:
            pair = slab(name, count=2)
            pltpu.make_async_copy(pair, pair, recv_sem.at[SLOT[name]]).wait()

    def arrived_half(sem):
        pltpu.make_async_copy(half("OWN"), half("OWN"), recv_sem.at[sem]).wait()

    def onward(name, there, device, count=1):
        send(slab(name, count=count), slab(there, count=count), there, SLOT[there], device, count=count)

    def relay(name, count=1):
        onward(name, name.replace("M", "O"), sibling, count)

    def along_z(name, count=1):
        onward(name, "MZ" + name[1:], z_near, count)

    barrier = pltpu.get_barrier_semaphore()
    greeted = [u_far, w_far, u_up, u_down, w_up, w_down, z_near, partner, sibling]
    for device in greeted:
        pl.semaphore_signal(barrier, inc=1, device_id=device, device_id_type=MESH)

    own_copy = pltpu.make_async_copy(lat_hbm, slab("OWN"), load_sem.at[4])
    loads = [
        pltpu.make_async_copy(q_hbm, q_ref, load_sem.at[0]),
        pltpu.make_async_copy(wk_hbm, wk_ref, load_sem.at[1]),
        pltpu.make_async_copy(wv_hbm, wv_ref, load_sem.at[2]),
        pltpu.make_async_copy(wo_hbm, wo_ref, load_sem.at[3]),
    ]
    own_copy.start()
    for load in loads:
        load.start()

    here = order_ref[ci]
    first_row = lax.broadcasted_iota(jnp.int32, (KDIM - C - R, SPAN), 0) == 0
    for name in ORDER:
        bias = jnp.where(order_ref[source(name)] <= here, 0.0, NEG)
        k_ref[C + R:, cols(SLOT[name])] = jnp.where(first_row, bias, 0.0).astype(BF16)
    token = lax.rem(lax.broadcasted_iota(jnp.int32, (TILE, SPAN), 0), SPAN)
    key = lax.broadcasted_iota(jnp.int32, (TILE, SPAN), 1)
    mask_ref[...] = jnp.where(key > token, NEG, 0.0)

    own_copy.wait()
    pl.semaphore_wait(barrier, len(greeted))
    onward("OWN", "M30", u_up)
    onward("OWN", "M10", u_down)
    onward("OWN", "Z00", z_near)
    onward("OWN", "M20", u_far)

    loads[0].wait()
    loads[1].wait()
    lane = lax.broadcasted_iota(jnp.int32, (SPAN, R), 1)
    one = jnp.where(lane == 0, 1.0, 0.0).astype(BF16)
    for h in range(HEADS):
        base = h * (NOPE + R)
        rows = slice(h * SPAN, (h + 1) * SPAN)
        qc_ref[rows, :C] = jnp.dot(
            q_ref[:, base:base + NOPE], wk_ref[h], preferred_element_type=F32
        ).astype(BF16)
        qc_ref[rows, C:] = jnp.concatenate([q_ref[:, base + NOPE:base + NOPE + R], one], axis=1)

    tiles = ROWS // TILE

    def chunk(index, events=None, after=None):
        events = events or {}
        first = SLOT[CHUNKS[index][0]]
        last = first + len(CHUNKS[index])
        width = (last - first) * SPAN
        keys = slice(first * SPAN, last * SPAN)
        begin = index == 0

        def rows_of(t):
            return pl.ds(t * TILE, TILE) if isinstance(t, int) else pl.ds(pl.multiple_of(t * TILE, TILE), TILE)

        def scores(t, b):
            s = jnp.dot(qc_ref[rows_of(t), :], k_ref[:, keys], preferred_element_type=F32)
            if begin:
                s = s + mask_ref[...]
            s_ref[b, :, :width] = s

        def soft(t, b):
            r = rows_of(t)
            s = s_ref[b, :, :width]
            top = jnp.max(s, axis=1, keepdims=True) * EXP_SCALE
            if begin:
                m_new = jnp.broadcast_to(top, (TILE, 128))
            else:
                m_old = m_ref[r, :]
                m_new = jnp.maximum(m_old, top)
                alpha = jnp.exp2(m_old - m_new)
                a_ref[b] = alpha
            wide = jnp.concatenate([m_new] * (width // 128), axis=1)
            e = jnp.exp2(s * EXP_SCALE - wide)
            part = e[:, :128]
            for i in range(1, width // 128):
                part = part + e[:, i * 128:(i + 1) * 128]
            l_ref[r, :] = part if begin else l_ref[r, :] * alpha + part
            m_ref[r, :] = m_new
            p_ref[b, :, :width] = e.astype(BF16)

        def values(t, b):
            r = rows_of(t)
            add = jnp.dot(p_ref[b, :, :width], kt_ref[:width, :], preferred_element_type=F32)
            if begin:
                acc_ref[r, :] = add
            else:
                acc_ref[r, :] = acc_ref[r, :] * jnp.concatenate([a_ref[b]] * 4, axis=1) + add

        kt_ref[:width, :] = k_ref[:C, keys].T
        for step in range(tiles + 2):
            if step in events:
                events[step]()
            if step < tiles:
                scores(step, step % 2)
            if 0 <= step - 1 < tiles:
                soft(step - 1, (step - 1) % 2)
            if 0 <= step - 2 < tiles:
                values(step - 2, step % 2)
                if after is not None:
                    after(step - 2)

    chunk(0)
    arrived("M10", "M30")
    onward("M10", "M13", w_up)
    onward("M30", "M31", w_down)
    along_z("M10", 2)
    relay("M10", 2)
    arrived("Z00")

    def two_away():
        arrived("M20")
        relay("M20")
        onward("M20", "M23", w_up)
        onward("M20", "M21", w_down)
        send(half("M20"), half("P22"), "P22", SLOT["P22"], w_far, HALF)
        along_z("M20")

    chunk(1, {2: two_away})
    arrived_pair("O10")
    arrived("O20")

    def diagonals():
        arrived("M13", "M31")
        relay("M13", 2)
        along_z("M13", 2)

    chunk(2, {4: diagonals})
    arrived_pair("MZ10")
    relay("MZ10", 2)

    def corners():
        arrived("M21", "M23")
        relay("M21", 2)
        along_z("M21", 2)
        arrived_half(SLOT["P22"])
        send(half("P22"), half("P22"), "P22r", P22_HALF, sibling, HALF)
        send(half("P22"), half("Z22"), "Z22", SLOT["Z22"], z_near, HALF)

    def z_two_away():
        arrived("MZ20")
        relay("MZ20")

    chunk(3, {3: corners, 4: z_two_away})
    arrived_pair("O13", "OZ10", "O21")

    def z_diagonals():
        arrived_pair("MZ13")
        relay("MZ13", 2)

    def z_corners():
        arrived_pair("MZ21")
        relay("MZ21", 2)

    def z_last():
        arrived_half(SLOT["Z22"])
        send(half("Z22"), half("Z22"), "Z22r", Z22_HALF, sibling, HALF)

    chunk(4, {3: z_diagonals, 5: z_corners})
    arrived_half(P22_HALF)
    arrived("OZ20")
    arrived_pair("OZ13")
    chunk(5, {2: z_last})
    arrived_half(Z22_HALF)
    arrived_pair("OZ21")
    loads[2].wait()

    def heads_of(t):
        for h in range(t * TILE // SPAN, (t + 1) * TILE // SPAN):
            rows = slice(h * SPAN, (h + 1) * SPAN)
            total = jnp.sum(l_ref[rows, :], axis=1, keepdims=True)
            mixed = (acc_ref[rows, :] / total).astype(BF16)
            ho_ref[:, h * V:(h + 1) * V] = jnp.dot(mixed, wv_ref[h], preferred_element_type=F32).astype(BF16)

    chunk(6, after=heads_of)
    loads[3].wait()

    pieces = ((0, 256), (256, 256), (512, 384))

    def project(zh, c, piece):
        at_col = pl.multiple_of((zh * 2 + c) * OWN_D + piece[0], 128)
        return jnp.dot(ho_ref[...], wo_ref[:, pl.ds(at_col, piece[1])], preferred_element_type=F32)

    def window(ref, piece):
        return ref.at[:, pl.ds(*piece)]

    def rs(src, dst, n, device):
        copy = pltpu.make_async_remote_copy(
            src_ref=src, dst_ref=dst, send_sem=rs_send.at[n], recv_sem=rs_recv.at[n],
            device_id=device, device_id_type=MESH,
        )
        copy.start()
        return copy

    far = s_ref.at[0, pl.ds(0, SPAN)]
    near = s_ref.at[1, pl.ds(0, SPAN)]
    count = len(pieces)
    copies_a, copies_b, copies_c = [], [], []
    for n, piece in enumerate(pieces):
        window(send_a, piece)[...] = project(1 - z_hi, 1 - core, piece).astype(BF16)
        copies_a.append(rs(window(send_a, piece), window(recv_a, piece), n, sibling))
    for piece in pieces:
        window(far, piece)[...] = project(1 - z_hi, core, piece)
    for n, piece in enumerate(pieces):
        copies_a[n].wait()
        window(send_b, piece)[...] = (window(far, piece)[...] + window(recv_a, piece)[...].astype(F32)).astype(BF16)
        copies_b.append(rs(window(send_b, piece), window(recv_b, piece), count + n, partner))
        window(send_c, piece)[...] = project(z_hi, 1 - core, piece).astype(BF16)
    copies_c.append(rs(send_c, recv_c, 2 * count, sibling))
    for piece in pieces:
        window(near, piece)[...] = project(z_hi, core, piece)
    copies_c[0].wait()
    for piece in pieces:
        window(near, piece)[...] = window(near, piece)[...] + window(recv_c, piece)[...].astype(F32)
    for number, rows, count in sends.values():
        sent = slab("OWN", 0, rows, count)
        pltpu.make_async_copy(sent, sent, send_sem.at[number]).wait()
    for n, piece in enumerate(pieces):
        copies_b[n].wait()
        out_ref[pl.ds(*piece), :] = (window(near, piece)[...] + window(recv_b, piece)[...].astype(F32)).T.astype(BF16)


def shards(queries, latents, w_key, w_value, w_out, block_order):
    any_spec = pl.BlockSpec(memory_space=pl.ANY)
    flops = 2 * ROWS * BLOCKS * SPAN * (KDIM + C)
    return pl.pallas_call(
        kernel,
        out_shape=jax.ShapeDtypeStruct((OWN_D, SPAN), BF16),
        in_specs=[any_spec] * 5 + [pl.BlockSpec(memory_space=pltpu.SMEM)],
        out_specs=pl.BlockSpec(memory_space=pltpu.VMEM),
        scratch_shapes=[
            pltpu.VMEM((SPAN, HEADS * (NOPE + R)), BF16),
            pltpu.VMEM((HEADS, NOPE, C), BF16),
            pltpu.VMEM((HEADS, C, V), BF16),
            pltpu.VMEM((HEADS * V, 4 * OWN_D), BF16),
            pltpu.VMEM((ROWS, KDIM), BF16),
            pltpu.VMEM((KDIM, BLOCKS * SPAN), BF16),
            pltpu.VMEM((WIDEST, C), BF16),
            pltpu.VMEM((TILE, SPAN), F32),
            pltpu.VMEM((ROWS, 128), F32),
            pltpu.VMEM((ROWS, 128), F32),
            pltpu.VMEM((ROWS, C), F32),
            pltpu.VMEM((2, TILE, WIDEST), F32),
            pltpu.VMEM((2, TILE, WIDEST), BF16),
            pltpu.VMEM((2, TILE, 128), F32),
            pltpu.VMEM((SPAN, HEADS * V), BF16),
        ] + [pltpu.VMEM((SPAN, OWN_D), BF16)] * 6 + [
            pltpu.SemaphoreType.DMA((5,)),
            pltpu.SemaphoreType.DMA((N_SEND,)),
            pltpu.SemaphoreType.DMA((N_RECV,)),
            pltpu.SemaphoreType.DMA((7,)),
            pltpu.SemaphoreType.DMA((7,)),
        ],
        compiler_params=pltpu.CompilerParams(
            collective_id=0, has_side_effects=True, vmem_limit_bytes=58 * 2**20
        ),
        cost_estimate=pl.CostEstimate(flops=flops, bytes_accessed=20 * 2**20, transcendentals=ROWS * BLOCKS * SPAN),
        name="latent_attention",
    )(queries, latents, w_key, w_value, w_out, block_order)


def solution(mesh):
    return jax.shard_map(
        shards,
        mesh=mesh,
        in_specs=(
            P("ctx", "head"),
            P(None, "ctx"),
            P("head", None, None),
            P("head", None, None),
            P("head", None),
            P(),
        ),
        out_specs=P("head", "ctx"),
        check_vma=False,
    )
```

```python
import functools
import math

import jax
import jax.numpy as jnp
from jax import lax
from jax.experimental import pallas as pl
from jax.experimental.pallas import tpu as pltpu
from jax.sharding import PartitionSpec as P

NOPE = 128
R = 64
C = 512
V = 128
HEADS = 16
SPAN = 128
ROWS = HEADS * SPAN
BLOCKS = 32
KDIM = 640
TILE = 512
OWN_D = 896
NEG = -1e30
EXP_SCALE = math.log2(math.e) / math.sqrt(NOPE + R)
MESH = pl.DeviceIdType.MESH
F32 = jnp.float32
BF16 = jnp.bfloat16

CHUNKS = (
    ("OWN",),
    ("Z00", "M10", "M30"),
    ("O10", "O30", "M20", "O20"),
    ("M13", "M31", "MZ10", "MZ30"),
    ("O13", "O31", "OZ10", "OZ30", "M21", "M23", "O21", "O23"),
    ("P22", "MZ20", "OZ20", "MZ13", "MZ31", "OZ13", "OZ31", "MZ21"),
    ("MZ23", "OZ21", "OZ23", "Z22"),
)
WIDEST = max(len(group) for group in CHUNKS) * 128
ORDER = [name for group in CHUNKS for name in group]
SLOT = {name: number for number, name in enumerate(ORDER)}
P22_HALF, Z22_HALF = BLOCKS, BLOCKS + 1
N_RECV = BLOCKS + 2
N_SEND = 48
HALF = (C + R) // 2


def kernel(
    q_hbm, lat_hbm, wk_hbm, wv_hbm, wo_hbm, order_ref, out_ref,
    q_ref, wk_ref, wv_ref, wo_ref, qc_ref, k_ref, kt_ref, mask_ref,
    m_ref, l_ref, acc_ref, s_ref, p_ref, a_ref, ho_ref,
    send_a, recv_a, send_b, recv_b, send_c, recv_c,
    load_sem, send_sem, recv_sem, rs_send, rs_recv,
):
    ci, hi = lax.axis_index("ctx"), lax.axis_index("head")
    z_lo, x, y = lax.div(ci, 16), lax.rem(lax.div(ci, 4), 4), lax.rem(ci, 4)
    z_hi, core = lax.div(hi, 2), lax.rem(hi, 2)
    sibling = (ci, z_hi * 2 + 1 - core)
    partner = (ci, (1 - z_hi) * 2 + core)
    z_near = ((1 - z_lo) * 16 + x * 4 + y, ((1 - core) * (1 - z_hi) + core * z_hi) * 2 + core)

    def place(along_core, z_low, du, dw):
        nx = lax.rem(x + (1 - along_core) * du + along_core * dw, 4)
        ny = lax.rem(y + (1 - along_core) * (4 - dw) + along_core * du, 4)
        return z_low * 16 + nx * 4 + ny

    def at(du, dw):
        return (place(core, z_lo, du, dw), hi)

    u_up, u_down, u_far = at(1, 0), at(3, 0), at(2, 0)
    w_up, w_down, w_far = at(0, 1), at(0, 3), at(0, 2)

    def source(name):
        if name == "OWN":
            return ci
        z_low = 1 - z_lo if "Z" in name else z_lo
        along = 1 - core if "O" in name else core
        return place(along, z_low, int(name[-2]), int(name[-1]))

    def cols(slot, count=1):
        return pl.ds(slot * SPAN, count * SPAN)

    def slab(name, first=0, rows=C + R, count=1):
        return k_ref.at[pl.ds(first, rows), cols(SLOT[name], count)]

    half_at = pl.multiple_of(core * HALF, 32)

    def half(name):
        return slab(name, half_at, HALF)

    sends = {}

    def send(src, dst, key, sem, device, rows=C + R, count=1):
        number = sends.setdefault(key, (len(sends), rows, count))[0]
        pltpu.make_async_remote_copy(
            src_ref=src, dst_ref=dst, send_sem=send_sem.at[number], recv_sem=recv_sem.at[sem],
            device_id=device, device_id_type=MESH,
        ).start()

    def arrived(*names):
        for name in names:
            pltpu.make_async_copy(slab(name), slab(name), recv_sem.at[SLOT[name]]).wait()

    def arrived_pair(*names):
        for name in names:
            pair = slab(name, count=2)
            pltpu.make_async_copy(pair, pair, recv_sem.at[SLOT[name]]).wait()

    def arrived_half(sem):
        pltpu.make_async_copy(half("OWN"), half("OWN"), recv_sem.at[sem]).wait()

    def onward(name, there, device, count=1):
        send(slab(name, count=count), slab(there, count=count), there, SLOT[there], device, count=count)

    def relay(name, count=1):
        onward(name, name.replace("M", "O"), sibling, count)

    def along_z(name, count=1):
        onward(name, "MZ" + name[1:], z_near, count)

    barrier = pltpu.get_barrier_semaphore()
    greeted = [u_far, w_far, u_up, u_down, w_up, w_down, z_near, partner, sibling]
    for device in greeted:
        pl.semaphore_signal(barrier, inc=1, device_id=device, device_id_type=MESH)

    own_copy = pltpu.make_async_copy(lat_hbm, slab("OWN"), load_sem.at[4])
    loads = [
        pltpu.make_async_copy(q_hbm, q_ref, load_sem.at[0]),
        pltpu.make_async_copy(wk_hbm, wk_ref, load_sem.at[1]),
        pltpu.make_async_copy(wv_hbm, wv_ref, load_sem.at[2]),
        pltpu.make_async_copy(wo_hbm, wo_ref, load_sem.at[3]),
    ]
    own_copy.start()
    for load in loads:
        load.start()

    here = order_ref[ci]
    first_row = lax.broadcasted_iota(jnp.int32, (KDIM - C - R, SPAN), 0) == 0
    for name in ORDER:
        bias = jnp.where(order_ref[source(name)] <= here, 0.0, NEG)
        k_ref[C + R:, cols(SLOT[name])] = jnp.where(first_row, bias, 0.0).astype(BF16)
    token = lax.rem(lax.broadcasted_iota(jnp.int32, (TILE, SPAN), 0), SPAN)
    key = lax.broadcasted_iota(jnp.int32, (TILE, SPAN), 1)
    mask_ref[...] = jnp.where(key > token, NEG, 0.0)

    own_copy.wait()
    pl.semaphore_wait(barrier, len(greeted))
    onward("OWN", "M30", u_up)
    onward("OWN", "M10", u_down)
    onward("OWN", "Z00", z_near)
    onward("OWN", "M20", u_far)

    loads[0].wait()
    loads[1].wait()
    lane = lax.broadcasted_iota(jnp.int32, (SPAN, R), 1)
    one = jnp.where(lane == 0, 1.0, 0.0).astype(BF16)
    for h in range(HEADS):
        base = h * (NOPE + R)
        rows = slice(h * SPAN, (h + 1) * SPAN)
        qc_ref[rows, :C] = jnp.dot(
            q_ref[:, base:base + NOPE], wk_ref[h], preferred_element_type=F32
        ).astype(BF16)
        qc_ref[rows, C:] = jnp.concatenate([q_ref[:, base + NOPE:base + NOPE + R], one], axis=1)

    tiles = ROWS // TILE

    def chunk(index, events=None, after=None):
        events = events or {}
        first = SLOT[CHUNKS[index][0]]
        last = first + len(CHUNKS[index])
        width = (last - first) * SPAN
        keys = slice(first * SPAN, last * SPAN)
        begin = index == 0

        def rows_of(t):
            return pl.ds(t * TILE, TILE) if isinstance(t, int) else pl.ds(pl.multiple_of(t * TILE, TILE), TILE)

        def scores(t, b):
            s = jnp.dot(qc_ref[rows_of(t), :], k_ref[:, keys], preferred_element_type=F32)
            if begin:
                s = s + mask_ref[...]
            s_ref[b, :, :width] = s

        def soft(t, b):
            r = rows_of(t)
            s = s_ref[b, :, :width]
            top = jnp.max(s, axis=1, keepdims=True) * EXP_SCALE
            if begin:
                m_new = jnp.broadcast_to(top, (TILE, 128))
            else:
                m_old = m_ref[r, :]
                m_new = jnp.maximum(m_old, top)
                alpha = jnp.exp2(m_old - m_new)
                a_ref[b] = alpha
            wide = jnp.concatenate([m_new] * (width // 128), axis=1)
            e = jnp.exp2(s * EXP_SCALE - wide)
            part = e[:, :128]
            for i in range(1, width // 128):
                part = part + e[:, i * 128:(i + 1) * 128]
            l_ref[r, :] = part if begin else l_ref[r, :] * alpha + part
            m_ref[r, :] = m_new
            p_ref[b, :, :width] = e.astype(BF16)

        def values(t, b):
            r = rows_of(t)
            add = jnp.dot(p_ref[b, :, :width], kt_ref[:width, :], preferred_element_type=F32)
            if begin:
                acc_ref[r, :] = add
            else:
                acc_ref[r, :] = acc_ref[r, :] * jnp.concatenate([a_ref[b]] * 4, axis=1) + add

        kt_ref[:width, :] = k_ref[:C, keys].T
        for step in range(tiles + 2):
            if step in events:
                events[step]()
            if step < tiles:
                scores(step, step % 2)
            if 0 <= step - 1 < tiles:
                soft(step - 1, (step - 1) % 2)
            if 0 <= step - 2 < tiles:
                values(step - 2, step % 2)
                if after is not None:
                    after(step - 2)

    chunk(0)
    arrived("M10", "M30")
    onward("M10", "M13", w_up)
    onward("M30", "M31", w_down)
    along_z("M10", 2)
    relay("M10", 2)
    arrived("Z00")

    def two_away():
        arrived("M20")
        relay("M20")
        onward("M20", "M23", w_up)
        onward("M20", "M21", w_down)
        send(half("M20"), half("P22"), "P22", SLOT["P22"], w_far, HALF)
        along_z("M20")

    chunk(1, {2: two_away})
    arrived_pair("O10")
    arrived("O20")

    def diagonals():
        arrived("M13", "M31")
        relay("M13", 2)
        along_z("M13", 2)

    chunk(2, {4: diagonals})
    arrived_pair("MZ10")
    relay("MZ10", 2)

    def corners():
        arrived("M21", "M23")
        relay("M21", 2)
        along_z("M21", 2)
        arrived_half(SLOT["P22"])
        send(half("P22"), half("P22"), "P22r", P22_HALF, sibling, HALF)
        send(half("P22"), half("Z22"), "Z22", SLOT["Z22"], z_near, HALF)

    def z_two_away():
        arrived("MZ20")
        relay("MZ20")

    chunk(3, {3: corners, 4: z_two_away})
    arrived_pair("O13", "OZ10", "O21")

    def z_diagonals():
        arrived_pair("MZ13")
        relay("MZ13", 2)

    def z_corners():
        arrived_pair("MZ21")
        relay("MZ21", 2)

    def z_last():
        arrived_half(SLOT["Z22"])
        send(half("Z22"), half("Z22"), "Z22r", Z22_HALF, sibling, HALF)

    chunk(4, {3: z_diagonals, 5: z_corners})
    arrived_half(P22_HALF)
    arrived("OZ20")
    arrived_pair("OZ13")
    chunk(5, {2: z_last})
    arrived_half(Z22_HALF)
    arrived_pair("OZ21")
    loads[2].wait()

    def heads_of(t):
        for h in range(t * TILE // SPAN, (t + 1) * TILE // SPAN):
            rows = slice(h * SPAN, (h + 1) * SPAN)
            total = jnp.sum(l_ref[rows, :], axis=1, keepdims=True)
            mixed = (acc_ref[rows, :] / total).astype(BF16)
            ho_ref[:, h * V:(h + 1) * V] = jnp.dot(mixed, wv_ref[h], preferred_element_type=F32).astype(BF16)

    chunk(6, after=heads_of)
    loads[3].wait()

    pieces = ((0, 256), (256, 256), (512, 384))

    def project(zh, c, piece):
        at_col = pl.multiple_of((zh * 2 + c) * OWN_D + piece[0], 128)
        return jnp.dot(ho_ref[...], wo_ref[:, pl.ds(at_col, piece[1])], preferred_element_type=F32)

    def window(ref, piece):
        return ref.at[:, pl.ds(*piece)]

    def rs(src, dst, n, device):
        copy = pltpu.make_async_remote_copy(
            src_ref=src, dst_ref=dst, send_sem=rs_send.at[n], recv_sem=rs_recv.at[n],
            device_id=device, device_id_type=MESH,
        )
        copy.start()
        return copy

    far = s_ref.at[0, pl.ds(0, SPAN)]
    near = s_ref.at[1, pl.ds(0, SPAN)]
    count = len(pieces)
    copies_a, copies_b, copies_c = [], [], []
    for n, piece in enumerate(pieces):
        window(send_a, piece)[...] = project(1 - z_hi, 1 - core, piece).astype(BF16)
        copies_a.append(rs(window(send_a, piece), window(recv_a, piece), n, sibling))
    for piece in pieces:
        window(far, piece)[...] = project(1 - z_hi, core, piece)
    for n, piece in enumerate(pieces):
        copies_a[n].wait()
        window(send_b, piece)[...] = (window(far, piece)[...] + window(recv_a, piece)[...].astype(F32)).astype(BF16)
        copies_b.append(rs(window(send_b, piece), window(recv_b, piece), count + n, partner))
        window(send_c, piece)[...] = project(z_hi, 1 - core, piece).astype(BF16)
    copies_c.append(rs(send_c, recv_c, 2 * count, sibling))
    for piece in pieces:
        window(near, piece)[...] = project(z_hi, core, piece)
    copies_c[0].wait()
    for piece in pieces:
        window(near, piece)[...] = window(near, piece)[...] + window(recv_c, piece)[...].astype(F32)
    for number, rows, count in sends.values():
        sent = slab("OWN", 0, rows, count)
        pltpu.make_async_copy(sent, sent, send_sem.at[number]).wait()
    for n, piece in enumerate(pieces):
        copies_b[n].wait()
        out_ref[pl.ds(*piece), :] = (window(near, piece)[...] + window(recv_b, piece)[...].astype(F32)).T.astype(BF16)


def shards(queries, latents, w_key, w_value, w_out, block_order):
    any_spec = pl.BlockSpec(memory_space=pl.ANY)
    flops = 2 * ROWS * BLOCKS * SPAN * (KDIM + C)
    return pl.pallas_call(
        kernel,
        out_shape=pltpu.VMEM((OWN_D, SPAN), BF16),
        in_specs=[any_spec] * 5 + [pl.BlockSpec(memory_space=pltpu.SMEM)],
        out_specs=pl.BlockSpec(memory_space=pltpu.VMEM),
        scratch_shapes=[
            pltpu.VMEM((SPAN, HEADS * (NOPE + R)), BF16),
            pltpu.VMEM((HEADS, NOPE, C), BF16),
            pltpu.VMEM((HEADS, C, V), BF16),
            pltpu.VMEM((HEADS * V, 4 * OWN_D), BF16),
            pltpu.VMEM((ROWS, KDIM), BF16),
            pltpu.VMEM((KDIM, BLOCKS * SPAN), BF16),
            pltpu.VMEM((WIDEST, C), BF16),
            pltpu.VMEM((TILE, SPAN), F32),
            pltpu.VMEM((ROWS, 128), F32),
            pltpu.VMEM((ROWS, 128), F32),
            pltpu.VMEM((ROWS, C), F32),
            pltpu.VMEM((2, TILE, WIDEST), F32),
            pltpu.VMEM((2, TILE, WIDEST), BF16),
            pltpu.VMEM((2, TILE, 128), F32),
            pltpu.VMEM((SPAN, HEADS * V), BF16),
        ] + [pltpu.VMEM((SPAN, OWN_D), BF16)] * 6 + [
            pltpu.SemaphoreType.DMA((5,)),
            pltpu.SemaphoreType.DMA((N_SEND,)),
            pltpu.SemaphoreType.DMA((N_RECV,)),
            pltpu.SemaphoreType.DMA((7,)),
            pltpu.SemaphoreType.DMA((7,)),
        ],
        compiler_params=pltpu.CompilerParams(
            collective_id=0, has_side_effects=True, vmem_limit_bytes=58 * 2**20
        ),
        cost_estimate=pl.CostEstimate(flops=flops, bytes_accessed=20 * 2**20, transcendentals=ROWS * BLOCKS * SPAN),
        name="latent_attention",
    )(queries, latents, w_key, w_value, w_out, block_order)


def solution(mesh):
    return jax.shard_map(
        shards,
        mesh=mesh,
        in_specs=(
            P("ctx", "head"),
            P(None, "ctx"),
            P("head", None, None),
            P("head", None, None),
            P("head", None),
            P(),
        ),
        out_specs=P("head", "ctx"),
        check_vma=False,
    )
```

```python
import functools
import math

import jax
import jax.numpy as jnp
from jax import lax
from jax.experimental import pallas as pl
from jax.experimental.pallas import tpu as pltpu
from jax.sharding import PartitionSpec as P

NOPE = 128
R = 64
C = 512
V = 128
HEADS = 16
SPAN = 128
ROWS = HEADS * SPAN
BLOCKS = 32
KDIM = 640
TILE = 512
OWN_D = 896
NEG = -1e30
EXP_SCALE = math.log2(math.e) / math.sqrt(NOPE + R)
MESH = pl.DeviceIdType.MESH
F32 = jnp.float32
BF16 = jnp.bfloat16

CHUNKS = (
    ("OWN",),
    ("Z00", "M10", "M30"),
    ("O10", "O30", "M20", "O20"),
    ("M13", "M31", "MZ10", "MZ30"),
    ("O13", "O31", "OZ10", "OZ30", "M21", "M23", "O21", "O23"),
    ("P22", "MZ20", "OZ20", "MZ13", "MZ31", "OZ13", "OZ31", "MZ21"),
    ("MZ23", "OZ21", "OZ23", "Z22"),
)
WIDEST = max(len(group) for group in CHUNKS) * 128
ORDER = [name for group in CHUNKS for name in group]
SLOT = {name: number for number, name in enumerate(ORDER)}
P22_HALF, Z22_HALF = BLOCKS, BLOCKS + 1
N_RECV = BLOCKS + 2
N_SEND = 48
HALF = (C + R) // 2


def kernel(
    q_hbm, lat_hbm, wk_hbm, wv_hbm, wo_hbm, order_ref, out_ref,
    q_ref, wk_ref, wv_ref, wo_ref, qc_ref, k_ref, kt_ref, mask_ref,
    m_ref, l_ref, acc_ref, s_ref, p_ref, a_ref, ho_ref,
    send_a, recv_a, send_b, recv_b, send_c, recv_c,
    load_sem, send_sem, recv_sem, rs_send, rs_recv,
):
    ci, hi = lax.axis_index("ctx"), lax.axis_index("head")
    z_lo, x, y = lax.div(ci, 16), lax.rem(lax.div(ci, 4), 4), lax.rem(ci, 4)
    z_hi, core = lax.div(hi, 2), lax.rem(hi, 2)
    sibling = (ci, z_hi * 2 + 1 - core)
    partner = (ci, (1 - z_hi) * 2 + core)
    z_near = ((1 - z_lo) * 16 + x * 4 + y, ((1 - core) * (1 - z_hi) + core * z_hi) * 2 + core)

    def place(along_core, z_low, du, dw):
        nx = lax.rem(x + (1 - along_core) * du + along_core * dw, 4)
        ny = lax.rem(y + (1 - along_core) * (4 - dw) + along_core * du, 4)
        return z_low * 16 + nx * 4 + ny

    def at(du, dw):
        return (place(core, z_lo, du, dw), hi)

    u_up, u_down, u_far = at(1, 0), at(3, 0), at(2, 0)
    w_up, w_down, w_far = at(0, 1), at(0, 3), at(0, 2)

    def source(name):
        if name == "OWN":
            return ci
        z_low = 1 - z_lo if "Z" in name else z_lo
        along = 1 - core if "O" in name else core
        return place(along, z_low, int(name[-2]), int(name[-1]))

    def cols(slot, count=1):
        return pl.ds(slot * SPAN, count * SPAN)

    def slab(name, first=0, rows=C + R, count=1):
        return k_ref.at[pl.ds(first, rows), cols(SLOT[name], count)]

    half_at = pl.multiple_of(core * HALF, 32)

    def half(name):
        return slab(name, half_at, HALF)

    sends = {}

    def send(src, dst, key, sem, device, rows=C + R, count=1):
        number = sends.setdefault(key, (len(sends), rows, count))[0]
        pltpu.make_async_remote_copy(
            src_ref=src, dst_ref=dst, send_sem=send_sem.at[number], recv_sem=recv_sem.at[sem],
            device_id=device, device_id_type=MESH,
        ).start()

    def arrived(*names):
        for name in names:
            pltpu.make_async_copy(slab(name), slab(name), recv_sem.at[SLOT[name]]).wait()

    def arrived_pair(*names):
        for name in names:
            pair = slab(name, count=2)
            pltpu.make_async_copy(pair, pair, recv_sem.at[SLOT[name]]).wait()

    def arrived_half(sem):
        pltpu.make_async_copy(half("OWN"), half("OWN"), recv_sem.at[sem]).wait()

    def onward(name, there, device, count=1):
        send(slab(name, count=count), slab(there, count=count), there, SLOT[there], device, count=count)

    def relay(name, count=1):
        onward(name, name.replace("M", "O"), sibling, count)

    def along_z(name, count=1):
        onward(name, "MZ" + name[1:], z_near, count)

    barrier = pltpu.get_barrier_semaphore()
    greeted = [u_far, w_far, u_up, u_down, w_up, w_down, z_near, partner, sibling]
    for device in greeted:
        pl.semaphore_signal(barrier, inc=1, device_id=device, device_id_type=MESH)

    own_copy = pltpu.make_async_copy(lat_hbm, slab("OWN"), load_sem.at[4])
    loads = [
        pltpu.make_async_copy(q_hbm, q_ref, load_sem.at[0]),
        pltpu.make_async_copy(wk_hbm, wk_ref, load_sem.at[1]),
        pltpu.make_async_copy(wv_hbm, wv_ref, load_sem.at[2]),
        pltpu.make_async_copy(wo_hbm, wo_ref, load_sem.at[3]),
    ]
    own_copy.start()
    for load in loads:
        load.start()

    here = order_ref[ci]
    first_row = lax.broadcasted_iota(jnp.int32, (KDIM - C - R, SPAN), 0) == 0
    for name in ORDER:
        bias = jnp.where(order_ref[source(name)] <= here, 0.0, NEG)
        k_ref[C + R:, cols(SLOT[name])] = jnp.where(first_row, bias, 0.0).astype(BF16)
    token = lax.rem(lax.broadcasted_iota(jnp.int32, (TILE, SPAN), 0), SPAN)
    key = lax.broadcasted_iota(jnp.int32, (TILE, SPAN), 1)
    mask_ref[...] = jnp.where(key > token, NEG, 0.0)

    own_copy.wait()
    pl.semaphore_wait(barrier, len(greeted))
    onward("OWN", "M30", u_up)
    onward("OWN", "M10", u_down)
    onward("OWN", "Z00", z_near)
    onward("OWN", "M20", u_far)

    loads[0].wait()
    loads[1].wait()
    lane = lax.broadcasted_iota(jnp.int32, (SPAN, R), 1)
    one = jnp.where(lane == 0, 1.0, 0.0).astype(BF16)
    for h in range(HEADS):
        base = h * (NOPE + R)
        rows = slice(h * SPAN, (h + 1) * SPAN)
        qc_ref[rows, :C] = jnp.dot(
            q_ref[:, base:base + NOPE], wk_ref[h], preferred_element_type=F32
        ).astype(BF16)
        qc_ref[rows, C:] = jnp.concatenate([q_ref[:, base + NOPE:base + NOPE + R], one], axis=1)

    tiles = ROWS // TILE

    def chunk(index, events=None, after=None):
        events = events or {}
        first = SLOT[CHUNKS[index][0]]
        last = first + len(CHUNKS[index])
        width = (last - first) * SPAN
        keys = slice(first * SPAN, last * SPAN)
        begin = index == 0

        def rows_of(t):
            return pl.ds(t * TILE, TILE) if isinstance(t, int) else pl.ds(pl.multiple_of(t * TILE, TILE), TILE)

        def scores(t, b):
            s = jnp.dot(qc_ref[rows_of(t), :], k_ref[:, keys], preferred_element_type=F32)
            if begin:
                s = s + mask_ref[...]
            s_ref[b, :, :width] = s

        def soft(t, b):
            r = rows_of(t)
            s = s_ref[b, :, :width]
            top = jnp.max(s, axis=1, keepdims=True) * EXP_SCALE
            if begin:
                m_new = jnp.broadcast_to(top, (TILE, 128))
            else:
                m_old = m_ref[r, :]
                m_new = jnp.maximum(m_old, top)
                alpha = jnp.exp2(m_old - m_new)
                a_ref[b] = alpha
            wide = jnp.concatenate([m_new] * (width // 128), axis=1)
            e = jnp.exp2(s * EXP_SCALE - wide)
            part = e[:, :128]
            for i in range(1, width // 128):
                part = part + e[:, i * 128:(i + 1) * 128]
            l_ref[r, :] = part if begin else l_ref[r, :] * alpha + part
            m_ref[r, :] = m_new
            p_ref[b, :, :width] = e.astype(BF16)

        def values(t, b):
            r = rows_of(t)
            add = jnp.dot(p_ref[b, :, :width], kt_ref[:width, :], preferred_element_type=F32)
            if begin:
                acc_ref[r, :] = add
            else:
                acc_ref[r, :] = acc_ref[r, :] * jnp.concatenate([a_ref[b]] * 4, axis=1) + add

        kt_ref[:width, :] = k_ref[:C, keys].T
        for step in range(tiles + 2):
            if step in events:
                events[step]()
            if step < tiles:
                scores(step, step % 2)
            if 0 <= step - 1 < tiles:
                soft(step - 1, (step - 1) % 2)
            if 0 <= step - 2 < tiles:
                values(step - 2, step % 2)
                if after is not None:
                    after(step - 2)

    chunk(0)
    arrived("M10", "M30")
    onward("M10", "M13", w_up)
    onward("M30", "M31", w_down)
    along_z("M10", 2)
    relay("M10", 2)
    arrived("Z00")

    def two_away():
        arrived("M20")
        relay("M20")
        onward("M20", "M23", w_up)
        onward("M20", "M21", w_down)
        send(half("M20"), half("P22"), "P22", SLOT["P22"], w_far, HALF)
        along_z("M20")

    chunk(1, {2: two_away})
    arrived_pair("O10")
    arrived("O20")

    def diagonals():
        arrived("M13", "M31")
        relay("M13", 2)
        along_z("M13", 2)

    chunk(2, {4: diagonals})
    arrived_pair("MZ10")
    relay("MZ10", 2)

    def corners():
        arrived("M21", "M23")
        relay("M21", 2)
        along_z("M21", 2)
        arrived_half(SLOT["P22"])
        send(half("P22"), half("P22"), "P22r", P22_HALF, sibling, HALF)
        send(half("P22"), half("Z22"), "Z22", SLOT["Z22"], z_near, HALF)

    def z_two_away():
        arrived("MZ20")
        relay("MZ20")

    chunk(3, {3: corners, 4: z_two_away})
    arrived_pair("O13", "OZ10", "O21")

    def z_diagonals():
        arrived_pair("MZ13")
        relay("MZ13", 2)

    def z_corners():
        arrived_pair("MZ21")
        relay("MZ21", 2)

    def z_last():
        arrived_half(SLOT["Z22"])
        send(half("Z22"), half("Z22"), "Z22r", Z22_HALF, sibling, HALF)

    chunk(4, {3: z_diagonals, 5: z_corners})
    arrived_half(P22_HALF)
    arrived("OZ20")
    arrived_pair("OZ13")
    chunk(5, {2: z_last})
    arrived_half(Z22_HALF)
    arrived_pair("OZ21")
    loads[2].wait()

    def heads_of(t):
        for h in range(t * TILE // SPAN, (t + 1) * TILE // SPAN):
            rows = slice(h * SPAN, (h + 1) * SPAN)
            inverse = 1.0 / jnp.sum(l_ref[rows, :], axis=1, keepdims=True)
            mixed = (acc_ref[rows, :] * inverse).astype(BF16)
            ho_ref[:, h * V:(h + 1) * V] = jnp.dot(mixed, wv_ref[h], preferred_element_type=F32).astype(BF16)

    chunk(6, after=heads_of)
    loads[3].wait()

    pieces = ((0, 256), (256, 384), (640, 256))

    def project(zh, c, piece):
        at_col = pl.multiple_of((zh * 2 + c) * OWN_D + piece[0], 128)
        return jnp.dot(ho_ref[...], wo_ref[:, pl.ds(at_col, piece[1])], preferred_element_type=F32)

    def window(ref, piece):
        return ref.at[:, pl.ds(*piece)]

    def rs(src, dst, n, device):
        copy = pltpu.make_async_remote_copy(
            src_ref=src, dst_ref=dst, send_sem=rs_send.at[n], recv_sem=rs_recv.at[n],
            device_id=device, device_id_type=MESH,
        )
        copy.start()
        return copy

    far = s_ref.at[0, pl.ds(0, SPAN)]
    near = s_ref.at[1, pl.ds(0, SPAN)]
    count = len(pieces)
    copies_a, copies_b, copies_c = [], [], []
    for n, piece in enumerate(pieces):
        window(send_a, piece)[...] = project(1 - z_hi, 1 - core, piece).astype(BF16)
        copies_a.append(rs(window(send_a, piece), window(recv_a, piece), n, sibling))
    for piece in pieces:
        window(far, piece)[...] = project(1 - z_hi, core, piece)
    for n, piece in enumerate(pieces):
        copies_a[n].wait()
        window(send_b, piece)[...] = (window(far, piece)[...] + window(recv_a, piece)[...].astype(F32)).astype(BF16)
        copies_b.append(rs(window(send_b, piece), window(recv_b, piece), count + n, partner))
        window(send_c, piece)[...] = project(z_hi, 1 - core, piece).astype(BF16)
    copies_c.append(rs(send_c, recv_c, 2 * count, sibling))
    for piece in pieces:
        window(near, piece)[...] = project(z_hi, core, piece)
    copies_c[0].wait()
    for piece in pieces:
        window(near, piece)[...] = window(near, piece)[...] + window(recv_c, piece)[...].astype(F32)
    for number, rows, count in sends.values():
        sent = slab("OWN", 0, rows, count)
        pltpu.make_async_copy(sent, sent, send_sem.at[number]).wait()
    for n, piece in enumerate(pieces):
        copies_b[n].wait()
        out_ref[pl.ds(*piece), :] = (window(near, piece)[...] + window(recv_b, piece)[...].astype(F32)).T.astype(BF16)


def shards(queries, latents, w_key, w_value, w_out, block_order):
    any_spec = pl.BlockSpec(memory_space=pl.ANY)
    flops = 2 * ROWS * BLOCKS * SPAN * (KDIM + C)
    return pl.pallas_call(
        kernel,
        out_shape=pltpu.VMEM((OWN_D, SPAN), BF16),
        in_specs=[any_spec] * 5 + [pl.BlockSpec(memory_space=pltpu.SMEM)],
        out_specs=pl.BlockSpec(memory_space=pltpu.VMEM),
        scratch_shapes=[
            pltpu.VMEM((SPAN, HEADS * (NOPE + R)), BF16),
            pltpu.VMEM((HEADS, NOPE, C), BF16),
            pltpu.VMEM((HEADS, C, V), BF16),
            pltpu.VMEM((HEADS * V, 4 * OWN_D), BF16),
            pltpu.VMEM((ROWS, KDIM), BF16),
            pltpu.VMEM((KDIM, BLOCKS * SPAN), BF16),
            pltpu.VMEM((WIDEST, C), BF16),
            pltpu.VMEM((TILE, SPAN), F32),
            pltpu.VMEM((ROWS, 128), F32),
            pltpu.VMEM((ROWS, 128), F32),
            pltpu.VMEM((ROWS, C), F32),
            pltpu.VMEM((2, TILE, WIDEST), F32),
            pltpu.VMEM((2, TILE, WIDEST), BF16),
            pltpu.VMEM((2, TILE, 128), F32),
            pltpu.VMEM((SPAN, HEADS * V), BF16),
        ] + [pltpu.VMEM((SPAN, OWN_D), BF16)] * 6 + [
            pltpu.SemaphoreType.DMA((5,)),
            pltpu.SemaphoreType.DMA((N_SEND,)),
            pltpu.SemaphoreType.DMA((N_RECV,)),
            pltpu.SemaphoreType.DMA((7,)),
            pltpu.SemaphoreType.DMA((7,)),
        ],
        compiler_params=pltpu.CompilerParams(
            collective_id=0, has_side_effects=True, vmem_limit_bytes=58 * 2**20
        ),
        cost_estimate=pl.CostEstimate(flops=flops, bytes_accessed=20 * 2**20, transcendentals=ROWS * BLOCKS * SPAN),
        name="latent_attention",
    )(queries, latents, w_key, w_value, w_out, block_order)


def solution(mesh):
    return jax.shard_map(
        shards,
        mesh=mesh,
        in_specs=(
            P("ctx", "head"),
            P(None, "ctx"),
            P("head", None, None),
            P("head", None, None),
            P("head", None),
            P(),
        ),
        out_specs=P("head", "ctx"),
        check_vma=False,
    )
```

```python
import functools
import math

import jax
import jax.numpy as jnp
from jax import lax
from jax.experimental import pallas as pl
from jax.experimental.pallas import tpu as pltpu
from jax.sharding import PartitionSpec as P

NOPE = 128
R = 64
C = 512
V = 128
HEADS = 16
SPAN = 128
ROWS = HEADS * SPAN
BLOCKS = 32
KDIM = 640
TILE = 512
OWN_D = 896
NEG = -1e30
EXP_SCALE = math.log2(math.e) / math.sqrt(NOPE + R)
MESH = pl.DeviceIdType.MESH
F32 = jnp.float32
BF16 = jnp.bfloat16

CHUNKS = (
    ("OWN",),
    ("Z00", "M10", "M30"),
    ("O10", "O30", "M20", "O20"),
    ("M13", "M31", "MZ10", "MZ30"),
    ("O13", "O31", "OZ10", "OZ30", "M21", "M23", "O21", "O23"),
    ("P22", "MZ20", "OZ20", "MZ13", "MZ31", "OZ13", "OZ31", "MZ21",
     "MZ23", "OZ21", "OZ23", "Z22"),
)
WIDEST = max(len(group) for group in CHUNKS) * 128
ORDER = [name for group in CHUNKS for name in group]
SLOT = {name: number for number, name in enumerate(ORDER)}
P22_HALF, Z22_HALF = BLOCKS, BLOCKS + 1
N_RECV = BLOCKS + 2
N_SEND = 48
HALF = (C + R) // 2


def kernel(
    q_hbm, lat_hbm, wk_hbm, wv_hbm, wo_hbm, order_ref, out_ref,
    q_ref, wk_ref, wv_ref, wo_ref, qc_ref, k_ref, kt_ref, mask_ref,
    m_ref, l_ref, acc_ref, s_ref, p_ref, a_ref, ho_ref,
    send_a, recv_a, send_b, recv_b, send_c, recv_c,
    load_sem, send_sem, recv_sem, rs_send, rs_recv,
):
    ci, hi = lax.axis_index("ctx"), lax.axis_index("head")
    z_lo, x, y = lax.div(ci, 16), lax.rem(lax.div(ci, 4), 4), lax.rem(ci, 4)
    z_hi, core = lax.div(hi, 2), lax.rem(hi, 2)
    sibling = (ci, z_hi * 2 + 1 - core)
    partner = (ci, (1 - z_hi) * 2 + core)
    z_near = ((1 - z_lo) * 16 + x * 4 + y, ((1 - core) * (1 - z_hi) + core * z_hi) * 2 + core)

    def place(along_core, z_low, du, dw):
        nx = lax.rem(x + (1 - along_core) * du + along_core * dw, 4)
        ny = lax.rem(y + (1 - along_core) * (4 - dw) + along_core * du, 4)
        return z_low * 16 + nx * 4 + ny

    def at(du, dw):
        return (place(core, z_lo, du, dw), hi)

    u_up, u_down, u_far = at(1, 0), at(3, 0), at(2, 0)
    w_up, w_down, w_far = at(0, 1), at(0, 3), at(0, 2)

    def source(name):
        if name == "OWN":
            return ci
        z_low = 1 - z_lo if "Z" in name else z_lo
        along = 1 - core if "O" in name else core
        return place(along, z_low, int(name[-2]), int(name[-1]))

    def cols(slot, count=1):
        return pl.ds(slot * SPAN, count * SPAN)

    def slab(name, first=0, rows=C + R, count=1):
        return k_ref.at[pl.ds(first, rows), cols(SLOT[name], count)]

    half_at = pl.multiple_of(core * HALF, 32)

    def half(name):
        return slab(name, half_at, HALF)

    sends = {}

    def send(src, dst, key, sem, device, rows=C + R, count=1):
        number = sends.setdefault(key, (len(sends), rows, count))[0]
        pltpu.make_async_remote_copy(
            src_ref=src, dst_ref=dst, send_sem=send_sem.at[number], recv_sem=recv_sem.at[sem],
            device_id=device, device_id_type=MESH,
        ).start()

    def arrived(*names):
        for name in names:
            pltpu.make_async_copy(slab(name), slab(name), recv_sem.at[SLOT[name]]).wait()

    def arrived_pair(*names):
        for name in names:
            pair = slab(name, count=2)
            pltpu.make_async_copy(pair, pair, recv_sem.at[SLOT[name]]).wait()

    def arrived_half(sem):
        pltpu.make_async_copy(half("OWN"), half("OWN"), recv_sem.at[sem]).wait()

    def onward(name, there, device, count=1):
        send(slab(name, count=count), slab(there, count=count), there, SLOT[there], device, count=count)

    def relay(name, count=1):
        onward(name, name.replace("M", "O"), sibling, count)

    def along_z(name, count=1):
        onward(name, "MZ" + name[1:], z_near, count)

    barrier = pltpu.get_barrier_semaphore()
    greeted = [u_far, w_far, u_up, u_down, w_up, w_down, z_near, partner, sibling]
    for device in greeted:
        pl.semaphore_signal(barrier, inc=1, device_id=device, device_id_type=MESH)

    own_copy = pltpu.make_async_copy(lat_hbm, slab("OWN"), load_sem.at[4])
    loads = [
        pltpu.make_async_copy(q_hbm, q_ref, load_sem.at[0]),
        pltpu.make_async_copy(wk_hbm, wk_ref, load_sem.at[1]),
        pltpu.make_async_copy(wv_hbm, wv_ref, load_sem.at[2]),
        pltpu.make_async_copy(wo_hbm, wo_ref, load_sem.at[3]),
    ]
    own_copy.start()
    for load in loads:
        load.start()

    here = order_ref[ci]
    first_row = lax.broadcasted_iota(jnp.int32, (KDIM - C - R, SPAN), 0) == 0
    for name in ORDER:
        bias = jnp.where(order_ref[source(name)] <= here, 0.0, NEG)
        k_ref[C + R:, cols(SLOT[name])] = jnp.where(first_row, bias, 0.0).astype(BF16)
    token = lax.rem(lax.broadcasted_iota(jnp.int32, (TILE, SPAN), 0), SPAN)
    key = lax.broadcasted_iota(jnp.int32, (TILE, SPAN), 1)
    mask_ref[...] = jnp.where(key > token, NEG, 0.0)

    own_copy.wait()
    pl.semaphore_wait(barrier, len(greeted))
    onward("OWN", "M30", u_up)
    onward("OWN", "M10", u_down)
    onward("OWN", "Z00", z_near)
    onward("OWN", "M20", u_far)

    loads[0].wait()
    loads[1].wait()
    lane = lax.broadcasted_iota(jnp.int32, (SPAN, R), 1)
    one = jnp.where(lane == 0, 1.0, 0.0).astype(BF16)
    for h in range(HEADS):
        base = h * (NOPE + R)
        rows = slice(h * SPAN, (h + 1) * SPAN)
        qc_ref[rows, :C] = jnp.dot(
            q_ref[:, base:base + NOPE], wk_ref[h], preferred_element_type=F32
        ).astype(BF16)
        qc_ref[rows, C:] = jnp.concatenate([q_ref[:, base + NOPE:base + NOPE + R], one], axis=1)

    tiles = ROWS // TILE

    def chunk(index, events=None, after=None):
        events = events or {}
        first = SLOT[CHUNKS[index][0]]
        last = first + len(CHUNKS[index])
        width = (last - first) * SPAN
        keys = slice(first * SPAN, last * SPAN)
        begin = index == 0

        def rows_of(t):
            return pl.ds(t * TILE, TILE) if isinstance(t, int) else pl.ds(pl.multiple_of(t * TILE, TILE), TILE)

        def scores(t, b):
            s = jnp.dot(qc_ref[rows_of(t), :], k_ref[:, keys], preferred_element_type=F32)
            if begin:
                s = s + mask_ref[...]
            s_ref[b, :, :width] = s

        def soft(t, b):
            r = rows_of(t)
            s = s_ref[b, :, :width]
            top = jnp.max(s, axis=1, keepdims=True) * EXP_SCALE
            if begin:
                m_new = jnp.broadcast_to(top, (TILE, 128))
            else:
                m_old = m_ref[r, :]
                m_new = jnp.maximum(m_old, top)
                alpha = jnp.exp2(m_old - m_new)
                a_ref[b] = alpha
            wide = jnp.concatenate([m_new] * (width // 128), axis=1)
            e = jnp.exp2(s * EXP_SCALE - wide)
            part = e[:, :128]
            for i in range(1, width // 128):
                part = part + e[:, i * 128:(i + 1) * 128]
            l_ref[r, :] = part if begin else l_ref[r, :] * alpha + part
            m_ref[r, :] = m_new
            p_ref[b, :, :width] = e.astype(BF16)

        def values(t, b):
            r = rows_of(t)
            add = jnp.dot(p_ref[b, :, :width], kt_ref[:width, :], preferred_element_type=F32)
            if begin:
                acc_ref[r, :] = add
            else:
                acc_ref[r, :] = acc_ref[r, :] * jnp.concatenate([a_ref[b]] * 4, axis=1) + add

        kt_ref[:width, :] = k_ref[:C, keys].T
        for step in range(tiles + 2):
            if step in events:
                events[step]()
            if step < tiles:
                scores(step, step % 2)
            if 0 <= step - 1 < tiles:
                soft(step - 1, (step - 1) % 2)
            if 0 <= step - 2 < tiles:
                values(step - 2, step % 2)
                if after is not None:
                    after(step - 2)

    chunk(0)
    arrived("M10", "M30")
    onward("M10", "M13", w_up)
    onward("M30", "M31", w_down)
    along_z("M10", 2)
    relay("M10", 2)
    arrived("Z00")

    def two_away():
        arrived("M20")
        relay("M20")
        onward("M20", "M23", w_up)
        onward("M20", "M21", w_down)
        send(half("M20"), half("P22"), "P22", SLOT["P22"], w_far, HALF)
        along_z("M20")

    chunk(1, {2: two_away})
    arrived_pair("O10")
    arrived("O20")

    def diagonals():
        arrived("M13", "M31")
        relay("M13", 2)
        along_z("M13", 2)

    chunk(2, {4: diagonals})
    arrived_pair("MZ10")
    relay("MZ10", 2)

    def corners():
        arrived("M21", "M23")
        relay("M21", 2)
        along_z("M21", 2)
        arrived_half(SLOT["P22"])
        send(half("P22"), half("P22"), "P22r", P22_HALF, sibling, HALF)
        send(half("P22"), half("Z22"), "Z22", SLOT["Z22"], z_near, HALF)

    def z_two_away():
        arrived("MZ20")
        relay("MZ20")

    chunk(3, {3: corners, 4: z_two_away})
    arrived_pair("O13", "OZ10", "O21")

    def z_diagonals():
        arrived_pair("MZ13")
        relay("MZ13", 2)

    def z_corners():
        arrived_pair("MZ21")
        relay("MZ21", 2)

    def z_last():
        arrived_half(SLOT["Z22"])
        send(half("Z22"), half("Z22"), "Z22r", Z22_HALF, sibling, HALF)

    chunk(4, {3: z_diagonals, 4: z_corners, 5: z_last})
    arrived_half(P22_HALF)
    arrived("OZ20")
    arrived_pair("OZ13")
    arrived_half(Z22_HALF)
    arrived_pair("OZ21")
    loads[2].wait()

    def heads_of(t):
        for h in range(t * TILE // SPAN, (t + 1) * TILE // SPAN):
            rows = slice(h * SPAN, (h + 1) * SPAN)
            inverse = 1.0 / jnp.sum(l_ref[rows, :], axis=1, keepdims=True)
            mixed = (acc_ref[rows, :] * inverse).astype(BF16)
            ho_ref[:, h * V:(h + 1) * V] = jnp.dot(mixed, wv_ref[h], preferred_element_type=F32).astype(BF16)

    chunk(5, after=heads_of)
    loads[3].wait()

    pieces = ((0, 256), (256, 384), (640, 256))

    def project(zh, c, piece):
        at_col = pl.multiple_of((zh * 2 + c) * OWN_D + piece[0], 128)
        return jnp.dot(ho_ref[...], wo_ref[:, pl.ds(at_col, piece[1])], preferred_element_type=F32)

    def window(ref, piece):
        return ref.at[:, pl.ds(*piece)]

    def rs(src, dst, n, device):
        copy = pltpu.make_async_remote_copy(
            src_ref=src, dst_ref=dst, send_sem=rs_send.at[n], recv_sem=rs_recv.at[n],
            device_id=device, device_id_type=MESH,
        )
        copy.start()
        return copy

    far = s_ref.at[0, pl.ds(0, SPAN)]
    near = s_ref.at[1, pl.ds(0, SPAN)]
    count = len(pieces)
    copies_a, copies_b, copies_c = [], [], []
    for n, piece in enumerate(pieces):
        window(send_a, piece)[...] = project(1 - z_hi, 1 - core, piece).astype(BF16)
        copies_a.append(rs(window(send_a, piece), window(recv_a, piece), n, sibling))
    for piece in pieces:
        window(far, piece)[...] = project(1 - z_hi, core, piece)
    for n, piece in enumerate(pieces):
        copies_a[n].wait()
        window(send_b, piece)[...] = (window(far, piece)[...] + window(recv_a, piece)[...].astype(F32)).astype(BF16)
        copies_b.append(rs(window(send_b, piece), window(recv_b, piece), count + n, partner))
        window(send_c, piece)[...] = project(z_hi, 1 - core, piece).astype(BF16)
    copies_c.append(rs(send_c, recv_c, 2 * count, sibling))
    for piece in pieces:
        window(near, piece)[...] = project(z_hi, core, piece)
    copies_c[0].wait()
    for piece in pieces:
        window(near, piece)[...] = window(near, piece)[...] + window(recv_c, piece)[...].astype(F32)
    for number, rows, count in sends.values():
        sent = slab("OWN", 0, rows, count)
        pltpu.make_async_copy(sent, sent, send_sem.at[number]).wait()
    for n, piece in enumerate(pieces):
        copies_b[n].wait()
        out_ref[pl.ds(*piece), :] = (window(near, piece)[...] + window(recv_b, piece)[...].astype(F32)).T.astype(BF16)


def shards(queries, latents, w_key, w_value, w_out, block_order):
    any_spec = pl.BlockSpec(memory_space=pl.ANY)
    flops = 2 * ROWS * BLOCKS * SPAN * (KDIM + C)
    return pl.pallas_call(
        kernel,
        out_shape=pltpu.VMEM((OWN_D, SPAN), BF16),
        in_specs=[any_spec] * 5 + [pl.BlockSpec(memory_space=pltpu.SMEM)],
        out_specs=pl.BlockSpec(memory_space=pltpu.VMEM),
        scratch_shapes=[
            pltpu.VMEM((SPAN, HEADS * (NOPE + R)), BF16),
            pltpu.VMEM((HEADS, NOPE, C), BF16),
            pltpu.VMEM((HEADS, C, V), BF16),
            pltpu.VMEM((HEADS * V, 4 * OWN_D), BF16),
            pltpu.VMEM((ROWS, KDIM), BF16),
            pltpu.VMEM((KDIM, BLOCKS * SPAN), BF16),
            pltpu.VMEM((WIDEST, C), BF16),
            pltpu.VMEM((TILE, SPAN), F32),
            pltpu.VMEM((ROWS, 128), F32),
            pltpu.VMEM((ROWS, 128), F32),
            pltpu.VMEM((ROWS, C), F32),
            pltpu.VMEM((2, TILE, WIDEST), F32),
            pltpu.VMEM((2, TILE, WIDEST), BF16),
            pltpu.VMEM((2, TILE, 128), F32),
            pltpu.VMEM((SPAN, HEADS * V), BF16),
        ] + [pltpu.VMEM((SPAN, OWN_D), BF16)] * 6 + [
            pltpu.SemaphoreType.DMA((5,)),
            pltpu.SemaphoreType.DMA((N_SEND,)),
            pltpu.SemaphoreType.DMA((N_RECV,)),
            pltpu.SemaphoreType.DMA((7,)),
            pltpu.SemaphoreType.DMA((7,)),
        ],
        compiler_params=pltpu.CompilerParams(
            collective_id=0, has_side_effects=True, vmem_limit_bytes=58 * 2**20
        ),
        cost_estimate=pl.CostEstimate(flops=flops, bytes_accessed=20 * 2**20, transcendentals=ROWS * BLOCKS * SPAN),
        name="latent_attention",
    )(queries, latents, w_key, w_value, w_out, block_order)


def solution(mesh):
    return jax.shard_map(
        shards,
        mesh=mesh,
        in_specs=(
            P("ctx", "head"),
            P(None, "ctx"),
            P("head", None, None),
            P("head", None, None),
            P("head", None),
            P(),
        ),
        out_specs=P("head", "ctx"),
        check_vma=False,
    )
```
